128 devices in a mesh: gx: 8 (over y, core), gy: 16 (over x, z).
Axes of the slice: x: 4, y: 4, z: 4, core: 2. Of those that a mesh axis runs over, the one named last changes fastest.
Arguments:
- multipoles: bfloat16 [64, 128, 32, 512], P('gx', 'gy'), may hold values from -6 to 6
- occupied: int32 [64, 128, 32], P('gx', 'gy'), may hold values from 0 to 1, as said below
- shift_matrices: bfloat16 [8, 512, 512], replicated, may hold values from -0.09375 to 0.09375
- compress: bfloat16 [512, 96], replicated, may hold values from -0.25 to 0.25
- kernels: bfloat16 [316, 96, 96], replicated, may hold values from -0.046875 to 0.046875
- expand: bfloat16 [96, 512], replicated, may hold values from -0.625 to 0.625
Outputs:
- local_expansions: float32 [64, 128, 32, 512], P('gx', 'gy')
The draws below stay inside these ranges and needn't reach their ends.
Inputs may be any that keep to these rules, and one draw needn't show every extreme that they name: 1 marks an occupied finest-level box, 0 an empty one; occupancy varies over the domain, and some level-4 boxes are empty as a whole.
All inputs are finite; a program needn't handle non-finite values.
Results may differ from the reference program's by a relative error of at most 0.0043.
Values may be sent and summed in bfloat16 or wider, within the bound.
A program may use at most 128 MiB of HBM per device.

```python
import jax
import jax.numpy as jnp
import numpy as np
from jax import lax

NZ = 32
P_SIZE = 512
R = 96
OFFSETS = 316
NX6 = 64
NY6 = 128


def draw_occupied(key, part):
    key = jax.random.fold_in(key, 17)
    key_x, key_y, key_roll, key_block = jax.random.split(key, 4)
    center_x = jax.random.randint(key_x, (), 0, NX6)
    center_y = jax.random.randint(key_y, (), 0, NY6)
    coord_x = jnp.arange(NX6, dtype=jnp.int32)[:, None]
    coord_y = jnp.arange(NY6, dtype=jnp.int32)[None, :]
    distance = jnp.abs(coord_x - center_x) + jnp.abs(coord_y - center_y)
    threshold = 900 - distance * 800 // (NX6 + NY6)
    rolls = jax.random.randint(key_roll, (NX6, NY6, NZ), 0, 1000)
    block_x = (jnp.arange(NX6 // 4, dtype=jnp.int32) * 4 + 2)[:, None]
    block_y = (jnp.arange(NY6 // 4, dtype=jnp.int32) * 4 + 2)[None, :]
    block_distance = jnp.abs(block_x - center_x) + jnp.abs(block_y - center_y)
    drop_level = block_distance * 600 // (NX6 + NY6)
    block_rolls = jax.random.randint(key_block, (NX6 // 4, NY6 // 4, NZ // 4), 0, 1000)
    keep_block = (block_rolls >= drop_level[:, :, None]).astype(jnp.int32)
    keep_fine = jnp.repeat(jnp.repeat(jnp.repeat(keep_block, 4, axis=0), 4, axis=1), 4, axis=2)
    return (rolls < threshold[:, :, None]).astype(jnp.int32) * keep_fine


def shard_levels(stream_key, shape, shards, smallest, high):
    gain, own = 1.0, jax.random.fold_in(stream_key, 6)
    for position, blocks in shards:
        steps = jnp.exp(jax.random.uniform(jax.random.fold_in(own, position), (blocks,), jnp.float32, smallest / len(shards), high / len(shards)))
        gain = gain * jnp.repeat(steps, shape[position] // blocks).reshape([-1 if axis == position else 1 for axis in range(len(shape))])
    return gain


def noise(key, dims, spread, reach, pieces=(), kind=jnp.bfloat16):
    values = jax.random.normal(key, dims, jnp.float32) * spread
    if len(pieces) > 0:
        values = shard_levels(key, dims, pieces, -0.22, 0.18) * values
    return jnp.clip(values, min=-reach, max=reach).astype(kind)


def setup_inputs(seed: int = 0) -> dict:
    key_list = jax.random.split(jax.random.key(seed), 7)
    multipoles = noise(key_list[0], (NX6, NY6, NZ, P_SIZE), 1.0, 6.0, ((0, 8), (1, 16)))
    occupied = draw_occupied(jax.random.fold_in(key_list[6], 71), 0)
    shift_matrices = noise(key_list[2], (8, P_SIZE, P_SIZE), (8 * P_SIZE) ** -0.5, 0.09375)
    compress = noise(key_list[3], (P_SIZE, R), P_SIZE ** -0.5, 0.25)
    kernels = noise(key_list[4], (OFFSETS, R, R), (189 * R) ** -0.5, 0.046875)
    expand = noise(key_list[5], (R, P_SIZE), R ** -0.5, 0.625)
    return {"multipoles": multipoles, "occupied": occupied, "shift_matrices": shift_matrices, "compress": compress, "kernels": kernels, "expand": expand}


def offset_list():
    offsets_found = []
    for a in range(-3, 4):
        for b in range(-3, 4):
            for c in range(-3, 4):
                if max(abs(a), abs(b), abs(c)) >= 2:
                    offsets_found.append((a, b, c))
    return offsets_found


def coarsen(occupancy):
    width_x, width_y, width_z = occupancy.shape
    return occupancy.reshape(width_x // 2, 2, width_y // 2, 2, width_z // 2, 2).max(axis=(1, 3, 5))


def ascend(moments, shift_matrices):
    width_x, width_y, width_z, coeffs = moments.shape
    summed = jnp.zeros(((width_x // 2) * (width_y // 2) * (width_z // 2), coeffs), jnp.float32)
    for child in range(8):
        child_rows = moments[child // 4::2, (child // 2) % 2::2, child % 2::2].reshape(-1, coeffs)
        summed = summed + jnp.dot(child_rows, shift_matrices[child], preferred_element_type=jnp.float32)
    return summed.reshape(width_x // 2, width_y // 2, width_z // 2, coeffs).astype(jnp.bfloat16)


def descend(parent, shift_matrices):
    width_x, width_y, width_z, coeffs = parent.shape
    flat_rows = parent.reshape(-1, coeffs)
    children = [jnp.dot(flat_rows, shift_matrices[child].T, preferred_element_type=jnp.float32) for child in range(8)]
    stacked = jnp.stack(children).reshape(2, 2, 2, width_x, width_y, width_z, coeffs)
    return stacked.transpose(3, 0, 4, 1, 5, 2, 6).reshape(2 * width_x, 2 * width_y, 2 * width_z, coeffs)


def squeeze_rank(moments, compress):
    width_x, width_y, width_z, coeffs = moments.shape
    charges = jnp.dot(moments.reshape(-1, coeffs), compress, preferred_element_type=jnp.float32)
    return charges.astype(jnp.bfloat16).reshape(width_x, width_y, width_z, compress.shape[1])


def far_field(charges, kernels):
    width_x, width_y, width_z, rank_size = charges.shape
    padded = jnp.pad(charges.astype(jnp.float32), ((3, 3), (3, 3), (3, 3), (0, 0)))
    offset_table = jnp.asarray(np.array(offset_list(), np.int32))
    parity_x = (jnp.arange(width_x) % 2).astype(jnp.int32)
    parity_y = (jnp.arange(width_y) % 2).astype(jnp.int32)
    parity_z = (jnp.arange(width_z) % 2).astype(jnp.int32)

    def step(accumulated, element):
        triple, kernel_rows = element
        window = lax.dynamic_slice(padded, (triple[0] + 3, triple[1] + 3, triple[2] + 3, jnp.int32(0)), (width_x, width_y, width_z, rank_size))
        product = jnp.dot(window.reshape(-1, rank_size), kernel_rows.astype(jnp.float32), precision=lax.Precision.HIGHEST)
        allow_x = (jnp.abs((parity_x + triple[0]) // 2) <= 1).astype(jnp.float32)
        allow_y = (jnp.abs((parity_y + triple[1]) // 2) <= 1).astype(jnp.float32)
        allow_z = (jnp.abs((parity_z + triple[2]) // 2) <= 1).astype(jnp.float32)
        allowed_mask = allow_x[:, None, None] * allow_y[None, :, None] * allow_z[None, None, :]
        return accumulated + product.reshape(width_x, width_y, width_z, rank_size) * allowed_mask[..., None], None

    start = jnp.zeros((width_x, width_y, width_z, rank_size), jnp.float32)
    accumulated, unused = lax.scan(step, start, (offset_table, kernels))
    return accumulated


def expand_out(far_terms, expand):
    width_x, width_y, width_z, rank_size = far_terms.shape
    rows = jnp.dot(far_terms.astype(jnp.bfloat16).reshape(-1, rank_size), expand, preferred_element_type=jnp.float32)
    return rows.reshape(width_x, width_y, width_z, expand.shape[1])


def reference(multipoles, occupied, shift_matrices, compress, kernels, expand):
    mask_fine = occupied
    mask_mid = coarsen(mask_fine)
    mask_top = coarsen(mask_mid)
    moments_fine = multipoles * mask_fine[..., None].astype(jnp.bfloat16)
    moments_mid = ascend(moments_fine, shift_matrices)
    moments_top = ascend(moments_mid, shift_matrices)
    far_top = far_field(squeeze_rank(moments_top, compress), kernels)
    far_mid = far_field(squeeze_rank(moments_mid, compress), kernels)
    far_fine = far_field(squeeze_rank(moments_fine, compress), kernels)
    local_top = mask_top[..., None].astype(jnp.float32) * expand_out(far_top, expand)
    local_mid = mask_mid[..., None].astype(jnp.float32) * (expand_out(far_mid, expand) + descend(local_top.astype(jnp.bfloat16), shift_matrices))
    local_fine = mask_fine[..., None].astype(jnp.float32) * (expand_out(far_fine, expand) + descend(local_mid.astype(jnp.bfloat16), shift_matrices))
    return local_fine
```

```python
import functools

import jax
import jax.numpy as jnp
import ml_dtypes
import numpy as np
from jax import lax
from jax.experimental import pallas as pl
from jax.experimental.pallas import tpu as pltpu
from jax.sharding import PartitionSpec as P

MESH = pl.DeviceIdType.MESH
F32, BF16 = jnp.float32, jnp.bfloat16
NC, RANK = 512, 96
BITS = [(c // 4, c // 2 % 2, c % 2) for c in range(8)]
DIRS = [(-1, 0), (1, 0), (0, -1), (0, 1), (-1, -1), (-1, 1), (1, -1), (1, 1)]
PACK = [32, 32, 32, 32, 16, 16, 16, 16]
PACK_AT = [0, 32, 64, 96, 128, 144, 160, 176]
SMALL_ROWS = 48
SHIFTS = [(a, b, c) for a in (-1, 0, 1) for b in (-1, 0, 1) for c in (-1, 0, 1) if (a, b, c) != (0, 0, 0)]


def dot(a, b):
    return jnp.dot(a, b, preferred_element_type=F32)


def dot_t(a, b):
    return lax.dot_general(a, b, (((1,), (1,)), ((), ())), preferred_element_type=F32)


def order_fine():
    p = np.zeros((256, 256), np.float32)
    for dy in range(2):
        for dz in range(2):
            for y in range(4):
                for z in range(16):
                    p[(dy * 2 + dz) * 64 + y * 16 + z, (2 * y + dy) * 32 + 2 * z + dz] = 1
    return p


def order_mid():
    p = np.zeros((256, 256), np.float32)
    for c, (dx, dy, dz) in enumerate(BITS):
        for x in range(2):
            for y in range(2):
                for z in range(8):
                    p[c * 32 + x * 16 + y * 8 + z, ((2 * x + dx) * 4 + 2 * y + dy) * 16 + 2 * z + dz] = 1
    return p


def order_top():
    p = np.zeros((128, 32), np.float32)
    for c, (dx, dy, dz) in enumerate(BITS):
        for z in range(4):
            p[c * 16 + z, (dx * 2 + dy) * 8 + 2 * z + dz] = 1
    return p


def packing():
    p = np.zeros((192, 48), np.float32)
    for (ex, ey), at in zip(DIRS, PACK_AT):
        if ex and ey:
            for z in range(8):
                p[at + z, (ex > 0) * 16 + (ey > 0) * 8 + z] = 1
            for z in range(4):
                p[at + 8 + z, 32 + z] = 1
        else:
            for w in range(2):
                for z in range(8):
                    x, y = ((ex > 0), w) if ex else (w, (ey > 0))
                    p[at + w * 8 + z, x * 16 + y * 8 + z] = 1
            for z in range(4):
                p[at + 16 + z, 32 + z] = 1
    return p


def windows_small():
    g = np.zeros((26, SMALL_ROWS, 240), np.float32)
    for i, (sx, sy, sz) in enumerate(SHIFTS):
        for x in range(2):
            for y in range(2):
                for z in range(8):
                    u, v, w = x + sx, y + sy, z + sz
                    if not 0 <= w < 8:
                        continue
                    ex, ey = (u > 1) - (u < 0), (v > 1) - (v < 0)
                    row = x * 16 + y * 8 + z
                    if not ex and not ey:
                        g[i, row, u * 16 + v * 8 + w] = 1
                        continue
                    at = 48 + PACK_AT[DIRS.index((-ex, -ey))]
                    g[i, row, at + (w if ex and ey else v * 8 + w if ex else u * 8 + w)] = 1
        for z in range(4):
            w = z + sz
            if not 0 <= w < 4:
                continue
            if not sx and not sy:
                g[i, 32 + z, 32 + w] = 1
            else:
                g[i, 32 + z, 48 + PACK_AT[DIRS.index((-sx, -sy))] + (8 if sx and sy else 16) + w] = 1
    return g.reshape(26 * SMALL_ROWS, 240)


def shift_z():
    p = np.zeros((2, 256, 256), np.float32)
    for k, s in enumerate((-1, 1)):
        for column in range(16):
            for z in range(16):
                if 0 <= z + s < 16:
                    p[k, column * 16 + z, column * 16 + z + s] = 1
    return p


def spread():
    e = np.zeros((RANK, 4 * 384), np.float32)
    for j in range(4):
        for r in range(RANK):
            e[r, j * 384 + j * RANK + r] = 1
    return e


def const(a):
    return jnp.asarray(a.astype(ml_dtypes.bfloat16))


def occupied_rows(occ_ref):
    return jnp.concatenate([occ_ref[:, y, :] for y in range(8)], axis=1).astype(F32)


def up_kernel(sizes, occ_ref, p6_ref, p5_ref, p4_ref, gs_ref, e_ref, comp_ref, x_hbm, s_hbm, h6, r54, xv, sv, mcat, wc, m54,
              msg, in_sem, send6, recv6, send54, recv54):
    gx, gy = lax.axis_index("gx"), lax.axis_index("gy")

    def there(ex, ey):
        ok = jnp.bool_(True)
        if ex:
            ok = (gx + ex >= 0) & (gx + ex < sizes[0])
        if ey:
            ok = ok & (gy + ey >= 0) & (gy + ey < sizes[1])
        return ok

    loads = [pltpu.make_async_copy(x_hbm.at[i], xv.at[i], in_sem.at[i]) for i in range(8)]
    loads.append(pltpu.make_async_copy(s_hbm, sv, in_sem.at[8]))
    for load in loads:
        load.start()

    zero = jnp.zeros((6, 16, 768), BF16)
    h6[0] = zero
    h6[5] = zero
    h6[1:5, 0] = zero[:4]
    h6[1:5, 5] = zero[:4]
    r54[48:240] = jnp.zeros((192, 768), BF16)
    barrier = pltpu.get_barrier_semaphore()
    for ex, ey in DIRS:
        @pl.when(there(ex, ey))
        def _():
            pl.semaphore_signal(barrier, inc=1, device_id=(gx + ex, gy + ey), device_id_type=MESH)

    for j in range(4):
        wc[j * NC:(j + 1) * NC] = dot(comp_ref[...], e_ref[:, j * 384:(j + 1) * 384]).astype(BF16)

    occ = occupied_rows(occ_ref)
    p6 = p6_ref[...].astype(F32)
    for x in range(8):
        loads[x].wait()
        masked = (p6 * occ[x:x + 1, :]).astype(BF16)
        rows = dot(masked, xv[x]).astype(BF16)
        for q in range(4):
            c = (x % 2) * 4 + q
            mcat[(x // 2) * 64:(x // 2) * 64 + 64, c * NC:(c + 1) * NC] = rows[q * 64:(q + 1) * 64]

    for h in range(2):
        charges = dot(mcat[:, h * 2048:(h + 1) * 2048], wc[...]).astype(BF16)
        h6[1:5, 1:5, :, h * 384:(h + 1) * 384] = charges.reshape(4, 4, 16, 384)

    pl.semaphore_wait(barrier, sum(jnp.where(there(ex, ey), 1, 0) for ex, ey in DIRS))

    def part(e):
        return pl.ds(1, 4) if e == 0 else 4 if e > 0 else 1

    def landing(e):
        return pl.ds(1, 4) if e == 0 else 0 if e > 0 else 5

    fine = []
    for d, (ex, ey) in enumerate(DIRS):
        fine.append(pltpu.make_async_remote_copy(
            src_ref=h6.at[part(ex), part(ey)], dst_ref=h6.at[landing(ex), landing(ey)], send_sem=send6.at[d],
            recv_sem=recv6.at[d], device_id=(gx + ex, gy + ey), device_id_type=MESH))

        @pl.when(there(ex, ey))
        def _():
            fine[d].start()

    loads[8].wait()
    shifts = sv[...].reshape(8 * NC, NC)
    mid = dot(mcat[...], shifts).astype(BF16)
    mid = dot(p5_ref[...], mid).astype(BF16)
    for c in range(8):
        m54[0:32, c * NC:(c + 1) * NC] = mid[c * 32:(c + 1) * 32]
    top = dot(m54[0:32], shifts).astype(BF16)
    top = dot(p4_ref[...], top).astype(BF16)
    for c in range(8):
        m54[32:48, c * NC:(c + 1) * NC] = top[c * 16:(c + 1) * 16]
    for h in range(2):
        r54[0:48, h * 384:(h + 1) * 384] = dot(m54[:, h * 2048:(h + 1) * 2048], wc[...]).astype(BF16)
    msg[...] = dot(gs_ref[...], r54[0:48]).astype(BF16)

    small = []
    for d, (ex, ey) in enumerate(DIRS):
        small.append(pltpu.make_async_remote_copy(
            src_ref=msg.at[pl.ds(PACK_AT[d], PACK[d])], dst_ref=r54.at[pl.ds(48 + PACK_AT[d], PACK[d])],
            send_sem=send54.at[d], recv_sem=recv54.at[d], device_id=(gx + ex, gy + ey), device_id_type=MESH))

        @pl.when(there(ex, ey))
        def _():
            small[d].start()

    for copies in (fine, small):
        for d, (ex, ey) in enumerate(DIRS):
            @pl.when(there(ex, ey))
            def _():
                copies[d].wait_send()

            @pl.when(there(-ex, -ey))
            def _():
                copies[d].wait_recv()


def slot_runs():
    runs, n = [], 0
    for slot in range(343):
        a, b, c = slot // 49 - 3, slot // 7 % 7 - 3, slot % 7 - 3
        if max(abs(a), abs(b), abs(c)) < 2:
            continue
        if runs and runs[-1][1] + runs[-1][2] == slot:
            runs[-1][2] += 1
        else:
            runs.append([n, slot, 1])
        n += 1
    return runs


INNER = [s for s in range(343) if max(abs(s // 49 - 3), abs(s // 7 % 7 - 3), abs(s % 7 - 3)) < 2]


def down_kernel(occ_ref, p6_ref, p5_ref, p5t_ref, p4t_ref, zs_ref, g_ref, exp_ref, h6, r54, kern_hbm, s_hbm, out_hbm, kv, kp, sv,
                hz, small, lhs, far, expp, mask6, mask5, mask4, mid_cm, mid_nat, ov, in_sem, out_sem):
    runs = slot_runs()
    loads = [pltpu.make_async_copy(kern_hbm.at[pl.ds(n, count)], kv.at[pl.ds(slot, count)], in_sem.at[i])
             for i, (n, slot, count) in enumerate(runs)]
    loads.append(pltpu.make_async_copy(s_hbm, sv, in_sem.at[len(runs)]))
    for load in loads:
        load.start()

    expp[...] = jnp.zeros_like(expp)
    expp[0:RANK] = exp_ref[...]
    far[...] = jnp.zeros_like(far)

    occ = occupied_rows(occ_ref)
    p6 = p6_ref[...].astype(F32)
    ones = jnp.ones((256, 128), BF16)
    for x in range(8):
        rows = dot((p6 * occ[x:x + 1, :]).astype(BF16), ones)
        for q in range(4):
            mask6[(x % 2) * 4 + q, (x // 2) * 64:(x // 2) * 64 + 64] = rows[q * 64:(q + 1) * 64]
    top5 = mask6[0]
    for c in range(1, 8):
        top5 = jnp.maximum(top5, mask6[c])
    mask5[...] = top5
    by_class = dot(p5_ref[...], top5.astype(BF16))
    top4 = by_class[0:32]
    for c in range(1, 8):
        top4 = jnp.maximum(top4, by_class[c * 32:(c + 1) * 32])
    mask4[...] = top4

    for first, count in ((0, 16), (16, 16), (32, 4)):
        block = h6[first * 16:(first + count) * 16]
        hz[1, first * 16:(first + count) * 16] = block
        for k in range(2):
            hz[2 * k, first * 16:(first + count) * 16] = dot(
                zs_ref[k, 0:count * 16, 0:count * 16], block).astype(BF16)
    for i in range(6):
        small[i * 208:(i + 1) * 208] = dot(g_ref[i * 208:(i + 1) * 208], r54[...]).astype(BF16)

    for load in loads[:-1]:
        load.wait()
    for slot in INNER:
        kv[slot] = jnp.zeros((RANK, RANK), BF16)

    @pl.loop(0, 343)
    def _(slot):
        kp[slot] = jnp.concatenate([kv[slot], jnp.zeros((RANK, 128 - RANK), BF16)], axis=1)

    @pl.loop(0, 26)
    def _(i):
        n = i + jnp.where(i >= 13, 1, 0)
        sx, sy, sz = n // 9, n // 3 % 3, n % 3
        for x in range(4):
            lhs[x * 64:(x + 1) * 64] = hz[sz, pl.ds(pl.multiple_of(((sx + x) * 6 + sy) * 16, 16), 64)]
        lhs[256:304] = small[pl.ds(pl.multiple_of(i * SMALL_ROWS, 16), SMALL_ROWS)]
        base = (2 * sx + 1) * 49 + (2 * sy + 1) * 7 + 2 * sz + 1
        for pair in range(4):
            rows = []
            for s in range(8):
                cols = []
                for t in (2 * pair, 2 * pair + 1):
                    delta = sum(w * (BITS[s][k] - BITS[t][k]) for k, w in enumerate((49, 7, 1)))
                    cols.append(kp[base + delta])
                rows.append(jnp.concatenate(cols, axis=1))
            far[:, pair * 256:(pair + 1) * 256] += dot(lhs[...], jnp.concatenate(rows, axis=0))

    loads[-1].wait()
    expand = expp[...]
    wide = lambda m: jnp.concatenate([m] * 4, axis=1)
    f4 = jnp.concatenate([far[288:304, c * 128:(c + 1) * 128] for c in range(8)], axis=0).astype(BF16)
    local4 = dot(p4t_ref[...], dot(f4, expand).astype(BF16))
    local4 = (local4 * wide(mask4[...])).astype(BF16)
    f5 = jnp.concatenate([far[256:288, c * 128:(c + 1) * 128] for c in range(8)], axis=0).astype(BF16)
    mid_far = dot(f5, expand)
    for c in range(8):
        mid_cm[c * 32:(c + 1) * 32] = (mid_far[c * 32:(c + 1) * 32] + dot_t(local4, sv[c])).astype(BF16)
    mid_nat[...] = (dot(p5t_ref[...], mid_cm[...]) * wide(mask5[...])).astype(BF16)
    stores = []
    for c, (dx, dy, dz) in enumerate(BITS):
        v = dot_t(mid_nat[...], sv[c]) + dot(far[0:256, c * 128:(c + 1) * 128].astype(BF16), expand)
        v = v * wide(mask6[c])
        for x in range(4):
            for y in range(4):
                for g in range(4):
                    ov[c // 2, g, x, y, pl.ds(dz, 16, stride=2), :] = v[(x * 4 + y) * 16:(x * 4 + y + 1) * 16,
                                                                       g * 128:(g + 1) * 128]
        if dz == 1:
            for g in range(4):
                stores.append(pltpu.make_async_copy(ov.at[c // 2, g], out_hbm.at[:, dx, :, dy, :, pl.ds(g * 128, 128)],
                                                    out_sem.at[c // 2 * 4 + g]))
                stores[-1].start()
    for store in stores:
        store.wait()


def full():
    return pl.BlockSpec(memory_space=pltpu.VMEM)


def anywhere():
    return pl.BlockSpec(memory_space=pl.ANY)


def per_device(sizes, multipoles, occupied, shift_matrices, compress, kernels, expand):
    x = multipoles.reshape(8, 256, NC)
    p5, p4 = order_mid(), order_top()
    dma = pltpu.SemaphoreType.DMA
    h6, r54 = pl.pallas_call(
        functools.partial(up_kernel, sizes),
        out_shape=(jax.ShapeDtypeStruct((6, 6, 16, 768), BF16), jax.ShapeDtypeStruct((240, 768), BF16)),
        in_specs=[full()] * 7 + [anywhere()] * 2,
        out_specs=(full(), full()),
        scratch_shapes=[
            pltpu.VMEM((8, 256, NC), BF16), pltpu.VMEM((8, NC, NC), BF16), pltpu.VMEM((256, 8 * NC), BF16),
            pltpu.VMEM((4 * NC, 384), BF16), pltpu.VMEM((48, 8 * NC), BF16), pltpu.VMEM((192, 768), BF16),
            dma((9,)), dma((8,)), dma((8,)), dma((8,)), dma((8,))],
        compiler_params=pltpu.CompilerParams(collective_id=0, has_side_effects=True, vmem_limit_bytes=40 * 2**20),
        name="up",
    )(occupied, const(order_fine()), const(p5), const(p4), const(packing()), const(spread()), compress, x, shift_matrices)

    out = pl.pallas_call(
        down_kernel,
        out_shape=jax.ShapeDtypeStruct((4, 2, 4, 2, 32, NC), F32),
        in_specs=[full()] * 10 + [anywhere()] * 2,
        out_specs=anywhere(),
        scratch_shapes=[
            pltpu.VMEM((343, RANK, RANK), BF16), pltpu.VMEM((343, RANK, 128), BF16), pltpu.VMEM((8, NC, NC), BF16),
            pltpu.VMEM((3, 576, 768), BF16), pltpu.VMEM((26 * SMALL_ROWS, 768), BF16), pltpu.VMEM((304, 768), BF16),
            pltpu.VMEM((304, 1024), F32), pltpu.VMEM((128, NC), BF16), pltpu.VMEM((8, 256, 128), F32),
            pltpu.VMEM((256, 128), F32), pltpu.VMEM((32, 128), F32), pltpu.VMEM((256, NC), BF16), pltpu.VMEM((256, NC), BF16),
            pltpu.VMEM((4, 4, 4, 4, 32, 128), F32), dma((16,)), dma((16,))],
        compiler_params=pltpu.CompilerParams(vmem_limit_bytes=56 * 2**20),
        name="down",
    )(occupied, const(order_fine()), const(p5), const(p5.T), const(p4.T), const(shift_z()), const(windows_small()), expand,
      h6.reshape(576, 768), r54, kernels, shift_matrices)
    return out.reshape(8, 8, 32, NC)


def solution(mesh):
    in_specs = (P("gx", "gy", None, None), P("gx", "gy", None), P(), P(), P(), P())
    out_specs = P("gx", "gy", None, None)
    sizes = (mesh.shape["gx"], mesh.shape["gy"])
    return jax.shard_map(
        functools.partial(per_device, sizes), mesh=mesh, in_specs=in_specs, out_specs=out_specs, check_vma=False
    )
```

```python
import functools

import jax
import jax.numpy as jnp
import ml_dtypes
import numpy as np
from jax import lax
from jax.experimental import pallas as pl
from jax.experimental.pallas import tpu as pltpu
from jax.sharding import PartitionSpec as P

MESH = pl.DeviceIdType.MESH
F32, BF16 = jnp.float32, jnp.bfloat16
NC, RANK = 512, 96
BITS = [(c // 4, c // 2 % 2, c % 2) for c in range(8)]
DIRS = [(-1, 0), (1, 0), (0, -1), (0, 1), (-1, -1), (-1, 1), (1, -1), (1, 1)]
PACK = [32, 32, 32, 32, 16, 16, 16, 16]
PACK_AT = [0, 32, 64, 96, 128, 144, 160, 176]
SMALL_ROWS = 48
STEP = 328
SHIFTS = [(a, b, c) for a in (-1, 0, 1) for b in (-1, 0, 1) for c in (-1, 0, 1) if (a, b, c) != (0, 0, 0)]


def dot(a, b):
    return jnp.dot(a, b, preferred_element_type=F32)


def dot_t(a, b):
    return lax.dot_general(a, b, (((1,), (1,)), ((), ())), preferred_element_type=F32)


def order_fine():
    p = np.zeros((256, 256), np.float32)
    for dy in range(2):
        for dz in range(2):
            for y in range(4):
                for z in range(16):
                    p[(dy * 2 + dz) * 64 + y * 16 + z, (2 * y + dy) * 32 + 2 * z + dz] = 1
    return p


def order_mid():
    p = np.zeros((256, 256), np.float32)
    for c, (dx, dy, dz) in enumerate(BITS):
        for x in range(2):
            for y in range(2):
                for z in range(8):
                    p[c * 32 + x * 16 + y * 8 + z, ((2 * x + dx) * 4 + 2 * y + dy) * 16 + 2 * z + dz] = 1
    return p


def order_top():
    p = np.zeros((128, 32), np.float32)
    for c, (dx, dy, dz) in enumerate(BITS):
        for z in range(4):
            p[c * 16 + z, (dx * 2 + dy) * 8 + 2 * z + dz] = 1
    return p


def packing():
    p = np.zeros((192, 48), np.float32)
    for (ex, ey), at in zip(DIRS, PACK_AT):
        if ex and ey:
            for z in range(8):
                p[at + z, (ex > 0) * 16 + (ey > 0) * 8 + z] = 1
            for z in range(4):
                p[at + 8 + z, 32 + z] = 1
        else:
            for w in range(2):
                for z in range(8):
                    x, y = ((ex > 0), w) if ex else (w, (ey > 0))
                    p[at + w * 8 + z, x * 16 + y * 8 + z] = 1
            for z in range(4):
                p[at + 16 + z, 32 + z] = 1
    return p


def windows_small():
    g = np.zeros((26, SMALL_ROWS, 240), np.float32)
    for i, (sx, sy, sz) in enumerate(SHIFTS):
        for x in range(2):
            for y in range(2):
                for z in range(8):
                    u, v, w = x + sx, y + sy, z + sz
                    if not 0 <= w < 8:
                        continue
                    ex, ey = (u > 1) - (u < 0), (v > 1) - (v < 0)
                    row = x * 16 + y * 8 + z
                    if not ex and not ey:
                        g[i, row, u * 16 + v * 8 + w] = 1
                        continue
                    at = 48 + PACK_AT[DIRS.index((-ex, -ey))]
                    g[i, row, at + (w if ex and ey else v * 8 + w if ex else u * 8 + w)] = 1
        for z in range(4):
            w = z + sz
            if not 0 <= w < 4:
                continue
            if not sx and not sy:
                g[i, 32 + z, 32 + w] = 1
            else:
                g[i, 32 + z, 48 + PACK_AT[DIRS.index((-sx, -sy))] + (8 if sx and sy else 16) + w] = 1
    return g.reshape(26 * SMALL_ROWS, 240)


def shift_z():
    p = np.zeros((2, 256, 256), np.float32)
    for k, s in enumerate((-1, 1)):
        for column in range(16):
            for z in range(16):
                if 0 <= z + s < 16:
                    p[k, column * 16 + z, column * 16 + z + s] = 1
    return p


def spread():
    e = np.zeros((RANK, 4 * 384), np.float32)
    for j in range(4):
        for r in range(RANK):
            e[r, j * 384 + j * RANK + r] = 1
    return e


def const(a):
    return jnp.asarray(a.astype(ml_dtypes.bfloat16))


def occupied_rows(occ_ref):
    return jnp.concatenate([occ_ref[:, y, :] for y in range(8)], axis=1).astype(F32)


def slot_runs():
    runs, n = [], 0
    for slot in range(343):
        a, b, c = slot // 49 - 3, slot // 7 % 7 - 3, slot % 7 - 3
        if max(abs(a), abs(b), abs(c)) < 2:
            continue
        if runs and runs[-1][1] + runs[-1][2] == slot:
            runs[-1][2] += 1
        else:
            runs.append([n, slot, 1])
        n += 1
    return runs


INNER = [s for s in range(343) if max(abs(s // 49 - 3), abs(s // 7 % 7 - 3), abs(s % 7 - 3)) < 2]


def start_all(pairs, sems, first=0):
    copies = [pltpu.make_async_copy(src, dst, sems.at[first + i]) for i, (src, dst) in enumerate(pairs)]
    for copy in copies:
        copy.start()
    return copies


def up_kernel(sizes, occ_hbm, p6_hbm, p5_hbm, p4_hbm, gs_hbm, e_hbm, comp_hbm, x_hbm, s_hbm, kt_hbm,
              h6, r54, kp, mask6, mask5, mask4,
              occ_ref, p6_ref, p5_ref, p4_ref, gs_ref, e_ref, comp_ref, xv, sv, kt, mcat, wc, m54, msg, turned,
              const_sem, in_sem, send6, recv6, send54, recv54):
    gx, gy = lax.axis_index("gx"), lax.axis_index("gy")

    def there(ex, ey):
        ok = jnp.bool_(True)
        if ex:
            ok = (gx + ex >= 0) & (gx + ex < sizes[0])
        if ey:
            ok = ok & (gy + ey >= 0) & (gy + ey < sizes[1])
        return ok

    consts = start_all([(comp_hbm, comp_ref), (e_hbm, e_ref), (occ_hbm, occ_ref), (p6_hbm, p6_ref)], const_sem)
    loads = start_all([(x_hbm.at[i], xv.at[i]) for i in range(8)] + [(s_hbm, sv)], in_sem)
    consts += start_all([(p5_hbm, p5_ref), (p4_hbm, p4_ref), (gs_hbm, gs_ref), (kt_hbm, kt)], const_sem, 4)

    zero = jnp.zeros((6, 16, 768), BF16)
    h6[0] = zero
    h6[5] = zero
    h6[1:5, 0] = zero[:4]
    h6[1:5, 5] = zero[:4]
    r54[48:240] = jnp.zeros((192, 768), BF16)
    barrier = pltpu.get_barrier_semaphore()
    for ex, ey in DIRS:
        @pl.when(there(ex, ey))
        def _():
            pl.semaphore_signal(barrier, inc=1, device_id=(gx + ex, gy + ey), device_id_type=MESH)

    for copy in consts[:4]:
        copy.wait()
    comp = comp_ref[...].astype(F32).T.astype(BF16)
    for j in range(4):
        wc[j * NC:(j + 1) * NC] = dot(comp, e_ref[:, j * 384:(j + 1) * 384]).astype(BF16)

    occ = occupied_rows(occ_ref)
    p6 = p6_ref[...].astype(F32)
    for x in range(8):
        loads[x].wait()
        masked = (p6 * occ[x:x + 1, :]).astype(BF16)
        rows = dot(masked, xv[x]).astype(BF16)
        for q in range(4):
            c = (x % 2) * 4 + q
            mcat[(x // 2) * 64:(x // 2) * 64 + 64, c * NC:(c + 1) * NC] = rows[q * 64:(q + 1) * 64]

    for h in range(2):
        charges = dot(mcat[:, h * 2048:(h + 1) * 2048], wc[...]).astype(BF16)
        h6[1:5, 1:5, :, h * 384:(h + 1) * 384] = charges.reshape(4, 4, 16, 384)

    pl.semaphore_wait(barrier, sum(jnp.where(there(ex, ey), 1, 0) for ex, ey in DIRS))

    def part(e):
        return pl.ds(1, 4) if e == 0 else 4 if e > 0 else 1

    def landing(e):
        return pl.ds(1, 4) if e == 0 else 0 if e > 0 else 5

    fine = []
    for d, (ex, ey) in enumerate(DIRS):
        fine.append(pltpu.make_async_remote_copy(
            src_ref=h6.at[part(ex), part(ey)], dst_ref=h6.at[landing(ex), landing(ey)], send_sem=send6.at[d],
            recv_sem=recv6.at[d], device_id=(gx + ex, gy + ey), device_id_type=MESH))

        @pl.when(there(ex, ey))
        def _():
            fine[d].start()

    loads[8].wait()
    for copy in consts[4:7]:
        copy.wait()
    shifts = sv[...].reshape(8 * NC, NC)
    mid = dot(mcat[...], shifts).astype(BF16)
    mid = dot(p5_ref[...], mid).astype(BF16)
    for c in range(8):
        m54[0:32, c * NC:(c + 1) * NC] = mid[c * 32:(c + 1) * 32]
    top = dot(m54[0:32], shifts).astype(BF16)
    top = dot(p4_ref[...], top).astype(BF16)
    for c in range(8):
        m54[32:48, c * NC:(c + 1) * NC] = top[c * 16:(c + 1) * 16]
    for h in range(2):
        r54[0:48, h * 384:(h + 1) * 384] = dot(m54[:, h * 2048:(h + 1) * 2048], wc[...]).astype(BF16)
    msg[...] = dot(gs_ref[...], r54[0:48]).astype(BF16)

    small = []
    for d, (ex, ey) in enumerate(DIRS):
        small.append(pltpu.make_async_remote_copy(
            src_ref=msg.at[pl.ds(PACK_AT[d], PACK[d])], dst_ref=r54.at[pl.ds(48 + PACK_AT[d], PACK[d])],
            send_sem=send54.at[d], recv_sem=recv54.at[d], device_id=(gx + ex, gy + ey), device_id_type=MESH))

        @pl.when(there(ex, ey))
        def _():
            small[d].start()

    ones = jnp.ones((256, 128), BF16)
    for x in range(8):
        rows = dot((p6 * occ[x:x + 1, :]).astype(BF16), ones)
        for q in range(4):
            mask6[(x % 2) * 4 + q, (x // 2) * 64:(x // 2) * 64 + 64] = rows[q * 64:(q + 1) * 64]
    top5 = mask6[0]
    for c in range(1, 8):
        top5 = jnp.maximum(top5, mask6[c])
    mask5[...] = top5
    by_class = dot(p5_ref[...], top5.astype(BF16))
    top4 = by_class[0:32]
    for c in range(1, 8):
        top4 = jnp.maximum(top4, by_class[c * 32:(c + 1) * 32])
    mask4[...] = top4

    consts[7].wait()

    @pl.loop(0, RANK, unroll=8)
    def _(r):
        v = jnp.concatenate([kt[r], jnp.zeros((128 - RANK, 316), BF16)], axis=0)
        v = jnp.concatenate([v, jnp.zeros((128, 68), BF16)], axis=1)
        turned[pl.ds(pl.multiple_of(r * STEP, 8), 320)] = v.T[:320].astype(F32)

    for n, slot, count in slot_runs():
        @pl.loop(0, count, unroll=4 if count == 4 else 8 if count == 32 else 6)
        def _(j):
            kp[slot + j] = turned[pl.ds(n + j, RANK, stride=STEP), :].astype(BF16)
    for slot in INNER:
        kp[slot] = jnp.zeros((RANK, 128), BF16)

    for copies in (fine, small):
        for d, (ex, ey) in enumerate(DIRS):
            @pl.when(there(ex, ey))
            def _():
                copies[d].wait_send()

            @pl.when(there(-ex, -ey))
            def _():
                copies[d].wait_recv()


def down_kernel(h6, r54, kp, mask6, mask5, mask4, zs_hbm, g_hbm, p4t_hbm, p5t_hbm, exp_hbm, s_hbm, out_hbm,
                zs_ref, g_ref, p4t_ref, p5t_ref, exp_ref, sv, hz, small, lhs, far, expp, mid_cm, mid_nat, ov,
                in_sem, out_sem):
    loads = start_all([(zs_hbm, zs_ref), (g_hbm, g_ref), (p4t_hbm, p4t_ref), (p5t_hbm, p5t_ref), (exp_hbm, exp_ref),
                       (s_hbm, sv)], in_sem)
    far[...] = jnp.zeros_like(far)
    loads[0].wait()
    loads[1].wait()

    for first, count in ((0, 16), (16, 16), (32, 4)):
        block = h6[first * 16:(first + count) * 16]
        hz[1, first * 16:(first + count) * 16] = block
        for k in range(2):
            hz[2 * k, first * 16:(first + count) * 16] = dot(
                zs_ref[k, 0:count * 16, 0:count * 16], block).astype(BF16)
    for i in range(6):
        small[i * 208:(i + 1) * 208] = dot(g_ref[i * 208:(i + 1) * 208], r54[...]).astype(BF16)

    @pl.loop(0, 26, unroll=2)
    def _(i):
        n = i + jnp.where(i >= 13, 1, 0)
        sx, sy, sz = n // 9, n // 3 % 3, n % 3
        for x in range(4):
            lhs[x * 64:(x + 1) * 64] = hz[sz, pl.ds(pl.multiple_of(((sx + x) * 6 + sy) * 16, 16), 64)]
        lhs[256:304] = small[pl.ds(pl.multiple_of(i * SMALL_ROWS, 16), SMALL_ROWS)]
        base = (2 * sx + 1) * 49 + (2 * sy + 1) * 7 + 2 * sz + 1
        for pair in range(4):
            rows = []
            for s in range(8):
                cols = []
                for t in (2 * pair, 2 * pair + 1):
                    delta = sum(w * (BITS[s][k] - BITS[t][k]) for k, w in enumerate((49, 7, 1)))
                    cols.append(kp[base + delta])
                rows.append(jnp.concatenate(cols, axis=1))
            far[:, pair * 256:(pair + 1) * 256] += dot(lhs[...], jnp.concatenate(rows, axis=0))

    for load in loads[2:]:
        load.wait()
    expp[...] = jnp.zeros_like(expp)
    expp[0:RANK] = exp_ref[...]
    expand = expp[...]
    wide = lambda m: jnp.concatenate([m] * 4, axis=1)
    f4 = jnp.concatenate([far[288:304, c * 128:(c + 1) * 128] for c in range(8)], axis=0).astype(BF16)
    local4 = dot(p4t_ref[...], dot(f4, expand).astype(BF16))
    local4 = (local4 * wide(mask4[...])).astype(BF16)
    f5 = jnp.concatenate([far[256:288, c * 128:(c + 1) * 128] for c in range(8)], axis=0).astype(BF16)
    mid_far = dot(f5, expand)
    for c in range(8):
        mid_cm[c * 32:(c + 1) * 32] = (mid_far[c * 32:(c + 1) * 32] + dot_t(local4, sv[c])).astype(BF16)
    mid_nat[...] = (dot(p5t_ref[...], mid_cm[...]) * wide(mask5[...])).astype(BF16)
    stores = []
    for c, (dx, dy, dz) in enumerate(BITS):
        v = dot_t(mid_nat[...], sv[c]) + dot(far[0:256, c * 128:(c + 1) * 128].astype(BF16), expand)
        v = v * wide(mask6[c])
        for x in range(4):
            for y in range(4):
                for g in range(4):
                    ov[c // 2, g, x, y, pl.ds(dz, 16, stride=2), :] = v[(x * 4 + y) * 16:(x * 4 + y + 1) * 16,
                                                                       g * 128:(g + 1) * 128]
        if dz == 1:
            for g in range(4):
                stores.append(pltpu.make_async_copy(ov.at[c // 2, g], out_hbm.at[:, dx, :, dy, :, pl.ds(g * 128, 128)],
                                                    out_sem.at[c // 2 * 4 + g]))
                stores[-1].start()
    for store in stores:
        store.wait()


def full():
    return pl.BlockSpec(memory_space=pltpu.VMEM)


def held(array):
    return pltpu.with_memory_space_constraint(array, pltpu.HBM)


def in_hbm():
    return pl.BlockSpec(memory_space=pltpu.HBM)


def per_device(sizes, multipoles, occupied, shift_matrices, compress, kernels, expand):
    x = multipoles.reshape(8, 256, NC)
    p5, p4 = order_mid(), order_top()
    dma, vmem, shape = pltpu.SemaphoreType.DMA, pltpu.VMEM, pltpu.VMEM
    kept = pl.pallas_call(
        functools.partial(up_kernel, sizes),
        out_shape=(shape((6, 6, 16, 768), BF16), shape((240, 768), BF16), shape((343, RANK, 128), BF16),
                   shape((8, 256, 128), F32), shape((256, 128), F32), shape((32, 128), F32)),
        in_specs=[in_hbm()] * 10,
        out_specs=(full(),) * 6,
        scratch_shapes=[
            vmem((8, 8, 32), jnp.int32), vmem((256, 256), BF16), vmem((256, 256), BF16), vmem((128, 32), BF16),
            vmem((192, 48), BF16), vmem((RANK, 1536), BF16), vmem((RANK, NC), BF16), vmem((8, 256, NC), BF16),
            vmem((8, NC, NC), BF16), vmem((RANK, RANK, 316), BF16), vmem((256, 8 * NC), BF16), vmem((4 * NC, 384), BF16),
            vmem((48, 8 * NC), BF16), vmem((192, 768), BF16), vmem((RANK * STEP, 128), F32),
            dma((8,)), dma((9,)), dma((8,)), dma((8,)), dma((8,)), dma((8,))],
        compiler_params=pltpu.CompilerParams(collective_id=0, has_side_effects=True, vmem_limit_bytes=44 * 2**20),
        name="up",
    )(*map(held, (occupied, const(order_fine()), const(p5), const(p4), const(packing()), const(spread()), compress.T, x,
                  shift_matrices, kernels.transpose(1, 2, 0))))

    out = pl.pallas_call(
        down_kernel,
        out_shape=jax.ShapeDtypeStruct((4, 2, 4, 2, 32, NC), F32),
        in_specs=[full()] * 6 + [in_hbm()] * 6,
        out_specs=in_hbm(),
        scratch_shapes=[
            vmem((2, 256, 256), BF16), vmem((26 * SMALL_ROWS, 240), BF16), vmem((32, 128), BF16), vmem((256, 256), BF16),
            vmem((RANK, NC), BF16), vmem((8, NC, NC), BF16),
            vmem((3, 576, 768), BF16), vmem((26 * SMALL_ROWS, 768), BF16), vmem((304, 768), BF16),
            vmem((304, 1024), F32), vmem((128, NC), BF16), vmem((256, NC), BF16), vmem((256, NC), BF16),
            vmem((4, 4, 4, 4, 32, 128), F32), dma((6,)), dma((16,))],
        compiler_params=pltpu.CompilerParams(vmem_limit_bytes=32 * 2**20),
        name="down",
    )(kept[0].reshape(576, 768), *kept[1:], *map(held, (const(shift_z()), const(windows_small()), const(p4.T), const(p5.T),
                                                        expand, shift_matrices)))
    return out.reshape(8, 8, 32, NC)


def solution(mesh):
    in_specs = (P("gx", "gy", None, None), P("gx", "gy", None), P(), P(), P(), P())
    out_specs = P("gx", "gy", None, None)
    sizes = (mesh.shape["gx"], mesh.shape["gy"])
    return jax.shard_map(
        functools.partial(per_device, sizes), mesh=mesh, in_specs=in_specs, out_specs=out_specs, check_vma=False
    )
```

```python
import functools

import jax
import jax.numpy as jnp
import ml_dtypes
import numpy as np
from jax import lax
from jax.experimental import pallas as pl
from jax.experimental.pallas import tpu as pltpu
from jax.sharding import PartitionSpec as P

MESH = pl.DeviceIdType.MESH
F32, BF16 = jnp.float32, jnp.bfloat16
NC, RANK = 512, 96
BITS = [(c // 4, c // 2 % 2, c % 2) for c in range(8)]
DIRS = [(-1, 0), (1, 0), (0, -1), (0, 1), (-1, -1), (-1, 1), (1, -1), (1, 1)]
PACK = [32, 32, 32, 32, 16, 16, 16, 16]
PACK_AT = [0, 32, 64, 96, 128, 144, 160, 176]
SMALL_ROWS = 48
STEP = 328
GROUP = 2
SECOND_AT = 0
SHIFTS = [(a, b, c) for a in (-1, 0, 1) for b in (-1, 0, 1) for c in (-1, 0, 1) if (a, b, c) != (0, 0, 0)]


def dot(a, b):
    return jnp.dot(a, b, preferred_element_type=F32)


def dot_t(a, b):
    return lax.dot_general(a, b, (((1,), (1,)), ((), ())), preferred_element_type=F32)


def order_fine():
    p = np.zeros((256, 256), np.float32)
    for dy in range(2):
        for dz in range(2):
            for y in range(4):
                for z in range(16):
                    p[(dy * 2 + dz) * 64 + y * 16 + z, (2 * y + dy) * 32 + 2 * z + dz] = 1
    return p


def order_mid():
    p = np.zeros((256, 256), np.float32)
    for c, (dx, dy, dz) in enumerate(BITS):
        for x in range(2):
            for y in range(2):
                for z in range(8):
                    p[c * 32 + x * 16 + y * 8 + z, ((2 * x + dx) * 4 + 2 * y + dy) * 16 + 2 * z + dz] = 1
    return p


def order_top():
    p = np.zeros((128, 32), np.float32)
    for c, (dx, dy, dz) in enumerate(BITS):
        for z in range(4):
            p[c * 16 + z, (dx * 2 + dy) * 8 + 2 * z + dz] = 1
    return p


def packing():
    p = np.zeros((192, 48), np.float32)
    for (ex, ey), at in zip(DIRS, PACK_AT):
        if ex and ey:
            for z in range(8):
                p[at + z, (ex > 0) * 16 + (ey > 0) * 8 + z] = 1
            for z in range(4):
                p[at + 8 + z, 32 + z] = 1
        else:
            for w in range(2):
                for z in range(8):
                    x, y = ((ex > 0), w) if ex else (w, (ey > 0))
                    p[at + w * 8 + z, x * 16 + y * 8 + z] = 1
            for z in range(4):
                p[at + 16 + z, 32 + z] = 1
    return p


def windows_small():
    g = np.zeros((26, SMALL_ROWS, 240), np.float32)
    for i, (sx, sy, sz) in enumerate(SHIFTS):
        for x in range(2):
            for y in range(2):
                for z in range(8):
                    u, v, w = x + sx, y + sy, z + sz
                    if not 0 <= w < 8:
                        continue
                    ex, ey = (u > 1) - (u < 0), (v > 1) - (v < 0)
                    row = x * 16 + y * 8 + z
                    if not ex and not ey:
                        g[i, row, u * 16 + v * 8 + w] = 1
                        continue
                    at = 48 + PACK_AT[DIRS.index((-ex, -ey))]
                    g[i, row, at + (w if ex and ey else v * 8 + w if ex else u * 8 + w)] = 1
        for z in range(4):
            w = z + sz
            if not 0 <= w < 4:
                continue
            if not sx and not sy:
                g[i, 32 + z, 32 + w] = 1
            else:
                g[i, 32 + z, 48 + PACK_AT[DIRS.index((-sx, -sy))] + (8 if sx and sy else 16) + w] = 1
    return g.reshape(26 * SMALL_ROWS, 240)


def shift_z():
    p = np.zeros((2, 256, 256), np.float32)
    for k, s in enumerate((-1, 1)):
        for column in range(16):
            for z in range(16):
                if 0 <= z + s < 16:
                    p[k, column * 16 + z, column * 16 + z + s] = 1
    return p


def const(a):
    return jnp.asarray(a.astype(ml_dtypes.bfloat16))


def occupied_rows(occ_ref):
    return jnp.concatenate([occ_ref[:, y, :] for y in range(8)], axis=1).astype(F32)


def slot_runs():
    runs, n = [], 0
    for slot in range(343):
        a, b, c = slot // 49 - 3, slot // 7 % 7 - 3, slot % 7 - 3
        if max(abs(a), abs(b), abs(c)) < 2:
            continue
        if runs and runs[-1][1] + runs[-1][2] == slot:
            runs[-1][2] += 1
        else:
            runs.append([n, slot, 1])
        n += 1
    return runs


INNER = [s for s in range(343) if max(abs(s // 49 - 3), abs(s // 7 % 7 - 3), abs(s % 7 - 3)) < 2]


def side_by_side(quad):
    v0, v1, v2, v3 = (v.astype(BF16).astype(F32) for v in quad)
    v1, v2, v3 = pltpu.roll(v1, 96, 1), pltpu.roll(v2, 64, 1), pltpu.roll(v3, 32, 1)
    lane = lax.broadcasted_iota(jnp.int32, v0.shape, 1)
    return jnp.concatenate([jnp.where(lane < 96, v0, v1), jnp.where(lane < 64, v1, v2), jnp.where(lane < 32, v2, v3)],
                           axis=1).astype(BF16)


def start_all(pairs, sems, first=0):
    copies = [pltpu.make_async_copy(src, dst, sems.at[first + i]) for i, (src, dst) in enumerate(pairs)]
    for copy in copies:
        copy.start()
    return copies


def up_kernel(sizes, occ_hbm, p6_hbm, p5_hbm, p4_hbm, gs_hbm, comp_hbm, x_hbm, s_hbm, kt_hbm,
              zs_hbm, g_hbm, p4t_hbm, p5t_hbm, exp_hbm,
              h6, r54, kp, mask6, mask5, mask4, zs_ref, g_ref, p4t_ref, p5t_ref, exp_ref, sv,
              occ_ref, p6_ref, p5_ref, p4_ref, gs_ref, comp_ref, xv, kt, mcat, comp, m5cat, msg, turned,
              const_sem, in_sem, kt_sem, send6, recv6, send54, recv54):
    gx, gy = lax.axis_index("gx"), lax.axis_index("gy")

    def there(ex, ey):
        ok = jnp.bool_(True)
        if ex:
            ok = (gx + ex >= 0) & (gx + ex < sizes[0])
        if ey:
            ok = ok & (gy + ey >= 0) & (gy + ey < sizes[1])
        return ok

    urgent = start_all([(comp_hbm, comp_ref), (occ_hbm, occ_ref), (p6_hbm, p6_ref)], const_sem)
    loads = start_all([(x_hbm.at[i], xv.at[i]) for i in range(8)], in_sem)

    zero = jnp.zeros((6, 16, 768), BF16)
    h6[0] = zero
    h6[5] = zero
    h6[1:5, 0] = zero[:4]
    h6[1:5, 5] = zero[:4]
    r54[48:240] = jnp.zeros((192, 768), BF16)
    barrier = pltpu.get_barrier_semaphore()
    for ex, ey in DIRS:
        @pl.when(there(ex, ey))
        def _():
            pl.semaphore_signal(barrier, inc=1, device_id=(gx + ex, gy + ey), device_id_type=MESH)

    for copy in urgent:
        copy.wait()
    comp[...] = jnp.concatenate([comp_ref[...].astype(F32), jnp.zeros((128 - RANK, NC), F32)], axis=0).T.astype(BF16)

    occ = occupied_rows(occ_ref)
    p6 = p6_ref[...].astype(F32)
    for x in range(8):
        loads[x].wait()
        if x == SECOND_AT:
            second = start_all([(s_hbm, sv), (p5_hbm, p5_ref), (p4_hbm, p4_ref), (gs_hbm, gs_ref)], const_sem, 3)
        masked = (p6 * occ[x:x + 1, :]).astype(BF16)
        rows = dot(masked, xv[x]).astype(BF16)
        for q in range(4):
            c = (x % 2) * 4 + q
            mcat[(x // 2) * 64:(x // 2) * 64 + 64, c * NC:(c + 1) * NC] = rows[q * 64:(q + 1) * 64]

    third = start_all([(kt_hbm.at[pl.ds(i * 16, 16)], kt.at[pl.ds(i * 16, 16)]) for i in range(6)], kt_sem)
    third += start_all([(zs_hbm, zs_ref), (g_hbm, g_ref), (p4t_hbm, p4t_ref), (p5t_hbm, p5t_ref),
                       (exp_hbm, exp_ref)], const_sem, 7)

    for h in range(2):
        charges = side_by_side([dot(mcat[:, c * NC:(c + 1) * NC], comp[...]) for c in range(4 * h, 4 * h + 4)])
        h6[1:5, 1:5, :, h * 384:(h + 1) * 384] = charges.reshape(4, 4, 16, 384)

    pl.semaphore_wait(barrier, sum(jnp.where(there(ex, ey), 1, 0) for ex, ey in DIRS))

    def part(e):
        return pl.ds(1, 4) if e == 0 else 4 if e > 0 else 1

    def landing(e):
        return pl.ds(1, 4) if e == 0 else 0 if e > 0 else 5

    fine = []
    for d, (ex, ey) in enumerate(DIRS):
        fine.append(pltpu.make_async_remote_copy(
            src_ref=h6.at[part(ex), part(ey)], dst_ref=h6.at[landing(ex), landing(ey)], send_sem=send6.at[d],
            recv_sem=recv6.at[d], device_id=(gx + ex, gy + ey), device_id_type=MESH))

        @pl.when(there(ex, ey))
        def _():
            fine[d].start()

    for copy in second:
        copy.wait()
    shifts = sv[...].reshape(8 * NC, NC)
    mid = dot(mcat[...], shifts).astype(BF16)
    mid = dot(p5_ref[...], mid).astype(BF16)
    for c in range(8):
        m5cat[:, c * NC:(c + 1) * NC] = mid[c * 32:(c + 1) * 32]
    q5 = dot(mid, comp[...])
    top = dot(m5cat[...], shifts).astype(BF16)
    top = dot(p4_ref[...], top).astype(BF16)
    q4 = dot(top, comp[...])
    for h in range(2):
        of = range(4 * h, 4 * h + 4)
        r54[0:32, h * 384:(h + 1) * 384] = side_by_side([q5[c * 32:(c + 1) * 32] for c in of])
        r54[32:48, h * 384:(h + 1) * 384] = side_by_side([q4[c * 16:(c + 1) * 16] for c in of])
    msg[...] = dot(gs_ref[...], r54[0:48]).astype(BF16)

    small = []
    for d, (ex, ey) in enumerate(DIRS):
        small.append(pltpu.make_async_remote_copy(
            src_ref=msg.at[pl.ds(PACK_AT[d], PACK[d])], dst_ref=r54.at[pl.ds(48 + PACK_AT[d], PACK[d])],
            send_sem=send54.at[d], recv_sem=recv54.at[d], device_id=(gx + ex, gy + ey), device_id_type=MESH))

        @pl.when(there(ex, ey))
        def _():
            small[d].start()

    ones = jnp.ones((256, 128), BF16)
    for x in range(8):
        rows = dot((p6 * occ[x:x + 1, :]).astype(BF16), ones)
        for q in range(4):
            mask6[(x % 2) * 4 + q, (x // 2) * 64:(x // 2) * 64 + 64] = rows[q * 64:(q + 1) * 64]
    top5 = mask6[0]
    for c in range(1, 8):
        top5 = jnp.maximum(top5, mask6[c])
    mask5[...] = top5
    by_class = dot(p5_ref[...], top5.astype(BF16))
    top4 = by_class[0:32]
    for c in range(1, 8):
        top4 = jnp.maximum(top4, by_class[c * 32:(c + 1) * 32])
    mask4[...] = top4

    for copy in third:
        copy.wait()

    @pl.loop(0, RANK, unroll=8)
    def _(r):
        v = jnp.concatenate([kt[r], jnp.zeros((128 - RANK, 316), BF16)], axis=0)
        v = jnp.concatenate([v, jnp.zeros((128, 68), BF16)], axis=1)
        turned[pl.ds(pl.multiple_of(r * STEP, 8), 320)] = v.T[:320].astype(F32)

    for n, slot, count in slot_runs():
        @pl.loop(0, count, unroll=4 if count == 4 else 8 if count == 32 else 6)
        def _(j):
            kp[slot + j] = turned[pl.ds(n + j, RANK, stride=STEP), :].astype(BF16)
    for slot in INNER:
        kp[slot] = jnp.zeros((RANK, 128), BF16)

    for copies in (fine, small):
        for d, (ex, ey) in enumerate(DIRS):
            @pl.when(there(ex, ey))
            def _():
                copies[d].wait_send()

            @pl.when(there(-ex, -ey))
            def _():
                copies[d].wait_recv()


def down_kernel(h6, r54, kp, mask6, mask5, mask4, zs_ref, g_ref, p4t_ref, p5t_ref, exp_ref, sv, out_hbm,
                hz, small, far, expp, mid_cm, mid_nat, ov, out_sem):

    for first, count in ((0, 16), (16, 16), (32, 4)):
        block = h6[first * 16:(first + count) * 16]
        hz[1, first * 16:(first + count) * 16] = block
        for k in range(2):
            hz[2 * k, first * 16:(first + count) * 16] = dot(
                zs_ref[k, 0:count * 16, 0:count * 16], block).astype(BF16)
    for i in range(6):
        small[i * 208:(i + 1) * 208] = dot(g_ref[i * 208:(i + 1) * 208], r54[...]).astype(BF16)

    def window(i):
        sx, sy, sz = (v + 1 for v in SHIFTS[i])
        parts = [hz[sz, ((sx + x) * 6 + sy) * 16:((sx + x) * 6 + sy) * 16 + 64] for x in range(4)]
        return jnp.concatenate(parts + [small[i * SMALL_ROWS:(i + 1) * SMALL_ROWS]], axis=0)

    def block(i, s, t):
        a, b, c = (2 * SHIFTS[i][k] + BITS[s][k] - BITS[t][k] for k in range(3))
        if max(abs(a), abs(b), abs(c)) < 2:
            return jnp.zeros((RANK, 128), BF16)
        return kp[(a + 3) * 49 + (b + 3) * 7 + c + 3]

    for first in range(0, 26, GROUP):
        together = range(first, first + GROUP)
        lhs = jnp.concatenate([window(i) for i in together], axis=1)
        for pair in range(4):
            rows = [jnp.concatenate([block(i, s, 2 * pair), block(i, s, 2 * pair + 1)], axis=1) for i in together for s in range(8)]
            product = dot(lhs, jnp.concatenate(rows, axis=0))
            if first:
                product += far[:, pair * 256:(pair + 1) * 256]
            far[:, pair * 256:(pair + 1) * 256] = product

    expp[...] = jnp.zeros_like(expp)
    expp[0:RANK] = exp_ref[...]
    expand = expp[...]
    wide = lambda m: jnp.concatenate([m] * 4, axis=1)
    f4 = jnp.concatenate([far[288:304, c * 128:(c + 1) * 128].astype(BF16) for c in range(8)], axis=0)
    local4 = dot(p4t_ref[...], dot(f4, expand).astype(BF16))
    local4 = (local4 * wide(mask4[...])).astype(BF16)
    f5 = jnp.concatenate([far[256:288, c * 128:(c + 1) * 128].astype(BF16) for c in range(8)], axis=0)
    mid_far = dot(f5, expand)
    for c in range(8):
        mid_cm[c * 32:(c + 1) * 32] = (mid_far[c * 32:(c + 1) * 32] + dot_t(local4, sv[c])).astype(BF16)
    mid_nat[...] = (dot(p5t_ref[...], mid_cm[...]) * wide(mask5[...])).astype(BF16)
    stores = []
    for c, (dx, dy, dz) in enumerate(BITS):
        v = dot_t(mid_nat[...], sv[c]) + dot(far[0:256, c * 128:(c + 1) * 128].astype(BF16), expand)
        v = v * wide(mask6[c])
        for x in range(4):
            for y in range(4):
                for g in range(4):
                    ov[c // 2, g, x, y, pl.ds(dz, 16, stride=2), :] = v[(x * 4 + y) * 16:(x * 4 + y + 1) * 16,
                                                                       g * 128:(g + 1) * 128]
        if dz == 1:
            for g in range(4):
                stores.append(pltpu.make_async_copy(ov.at[c // 2, g], out_hbm.at[:, dx, :, dy, :, pl.ds(g * 128, 128)],
                                                    out_sem.at[c // 2 * 4 + g]))
                stores[-1].start()
    for store in stores:
        store.wait()


def full():
    return pl.BlockSpec(memory_space=pltpu.VMEM)


def held(array):
    return pltpu.with_memory_space_constraint(array, pltpu.HBM)


def in_hbm():
    return pl.BlockSpec(memory_space=pltpu.HBM)


def per_device(sizes, multipoles, occupied, shift_matrices, compress, kernels, expand):
    x = multipoles.reshape(8, 256, NC)
    p5, p4 = order_mid(), order_top()
    dma, vmem, shape = pltpu.SemaphoreType.DMA, pltpu.VMEM, pltpu.VMEM
    kept = pl.pallas_call(
        functools.partial(up_kernel, sizes),
        out_shape=(shape((6, 6, 16, 768), BF16), shape((240, 768), BF16), shape((343, RANK, 128), BF16),
                   shape((8, 256, 128), F32), shape((256, 128), F32), shape((32, 128), F32),
                   shape((2, 256, 256), BF16), shape((26 * SMALL_ROWS, 240), BF16), shape((32, 128), BF16),
                   shape((256, 256), BF16), shape((RANK, NC), BF16), shape((8, NC, NC), BF16)),
        in_specs=[in_hbm()] * 14,
        out_specs=(full(),) * 12,
        scratch_shapes=[
            vmem((8, 8, 32), jnp.int32), vmem((256, 256), BF16), vmem((256, 256), BF16), vmem((128, 32), BF16),
            vmem((192, 48), BF16), vmem((RANK, NC), BF16), vmem((8, 256, NC), BF16),
            vmem((RANK, RANK, 316), BF16), vmem((256, 8 * NC), BF16), vmem((NC, 128), BF16),
            vmem((32, 8 * NC), BF16), vmem((192, 768), BF16), vmem((RANK * STEP, 128), F32),
            dma((12,)), dma((8,)), dma((6,)), dma((8,)), dma((8,)), dma((8,)), dma((8,))],
        compiler_params=pltpu.CompilerParams(collective_id=0, has_side_effects=True, vmem_limit_bytes=34 * 2**20),
        name="up",
    )(*map(held, (occupied, const(order_fine()), const(p5), const(p4), const(packing()), compress.T, x,
                  shift_matrices, kernels.transpose(1, 2, 0), const(shift_z()), const(windows_small()), const(p4.T),
                  const(p5.T), expand)))

    out = pl.pallas_call(
        down_kernel,
        out_shape=jax.ShapeDtypeStruct((4, 2, 4, 2, 32, NC), F32),
        in_specs=[full()] * 12,
        out_specs=in_hbm(),
        scratch_shapes=[
            vmem((3, 576, 768), BF16), vmem((26 * SMALL_ROWS, 768), BF16), vmem((304, 1024), F32), vmem((128, NC), BF16), vmem((256, NC), BF16),
            vmem((256, NC), BF16), vmem((4, 4, 4, 4, 32, 128), F32), dma((16,))],
        compiler_params=pltpu.CompilerParams(vmem_limit_bytes=24 * 2**20),
        name="down",
    )(kept[0].reshape(576, 768), *kept[1:])
    return out.reshape(8, 8, 32, NC)


def solution(mesh):
    in_specs = (P("gx", "gy", None, None), P("gx", "gy", None), P(), P(), P(), P())
    out_specs = P("gx", "gy", None, None)
    sizes = (mesh.shape["gx"], mesh.shape["gy"])
    return jax.shard_map(
        functools.partial(per_device, sizes), mesh=mesh, in_specs=in_specs, out_specs=out_specs, check_vma=False
    )
```

```python
import functools

import jax
import jax.numpy as jnp
import ml_dtypes
import numpy as np
from jax import lax
from jax.experimental import pallas as pl
from jax.experimental.pallas import tpu as pltpu
from jax.sharding import PartitionSpec as P

MESH = pl.DeviceIdType.MESH
F32, BF16 = jnp.float32, jnp.bfloat16
NC, RANK = 512, 96
BITS = [(c // 4, c // 2 % 2, c % 2) for c in range(8)]
DIRS = [(-1, 0), (1, 0), (0, -1), (0, 1), (-1, -1), (-1, 1), (1, -1), (1, 1)]
PACK = [32, 32, 32, 32, 16, 16, 16, 16]
PACK_AT = [0, 32, 64, 96, 128, 144, 160, 176]
SMALL_ROWS = 48
STEP = 328
GROUP = 2
SECOND_AT = 0
SHIFTS = [(a, b, c) for a in (-1, 0, 1) for b in (-1, 0, 1) for c in (-1, 0, 1) if (a, b, c) != (0, 0, 0)]


def dot(a, b):
    return jnp.dot(a, b, preferred_element_type=F32)


def dot_t(a, b):
    return lax.dot_general(a, b, (((1,), (1,)), ((), ())), preferred_element_type=F32)


def order_fine():
    p = np.zeros((256, 256), np.float32)
    for dy in range(2):
        for dz in range(2):
            for y in range(4):
                for z in range(16):
                    p[(dy * 2 + dz) * 64 + y * 16 + z, (2 * y + dy) * 32 + 2 * z + dz] = 1
    return p


def order_mid():
    p = np.zeros((256, 256), np.float32)
    for c, (dx, dy, dz) in enumerate(BITS):
        for x in range(2):
            for y in range(2):
                for z in range(8):
                    p[c * 32 + x * 16 + y * 8 + z, ((2 * x + dx) * 4 + 2 * y + dy) * 16 + 2 * z + dz] = 1
    return p


def order_top():
    p = np.zeros((128, 32), np.float32)
    for c, (dx, dy, dz) in enumerate(BITS):
        for z in range(4):
            p[c * 16 + z, (dx * 2 + dy) * 8 + 2 * z + dz] = 1
    return p


def packing():
    p = np.zeros((192, 48), np.float32)
    for (ex, ey), at in zip(DIRS, PACK_AT):
        if ex and ey:
            for z in range(8):
                p[at + z, (ex > 0) * 16 + (ey > 0) * 8 + z] = 1
            for z in range(4):
                p[at + 8 + z, 32 + z] = 1
        else:
            for w in range(2):
                for z in range(8):
                    x, y = ((ex > 0), w) if ex else (w, (ey > 0))
                    p[at + w * 8 + z, x * 16 + y * 8 + z] = 1
            for z in range(4):
                p[at + 16 + z, 32 + z] = 1
    return p


def windows_small():
    g = np.zeros((26, SMALL_ROWS, 240), np.float32)
    for i, (sx, sy, sz) in enumerate(SHIFTS):
        for x in range(2):
            for y in range(2):
                for z in range(8):
                    u, v, w = x + sx, y + sy, z + sz
                    if not 0 <= w < 8:
                        continue
                    ex, ey = (u > 1) - (u < 0), (v > 1) - (v < 0)
                    row = x * 16 + y * 8 + z
                    if not ex and not ey:
                        g[i, row, u * 16 + v * 8 + w] = 1
                        continue
                    at = 48 + PACK_AT[DIRS.index((-ex, -ey))]
                    g[i, row, at + (w if ex and ey else v * 8 + w if ex else u * 8 + w)] = 1
        for z in range(4):
            w = z + sz
            if not 0 <= w < 4:
                continue
            if not sx and not sy:
                g[i, 32 + z, 32 + w] = 1
            else:
                g[i, 32 + z, 48 + PACK_AT[DIRS.index((-sx, -sy))] + (8 if sx and sy else 16) + w] = 1
    return g.reshape(26 * SMALL_ROWS, 240)


def shift_z():
    p = np.zeros((2, 256, 256), np.float32)
    for k, s in enumerate((-1, 1)):
        for column in range(16):
            for z in range(16):
                if 0 <= z + s < 16:
                    p[k, column * 16 + z, column * 16 + z + s] = 1
    return p


def const(a):
    return jnp.asarray(a.astype(ml_dtypes.bfloat16))


def occupied_rows(occ_ref):
    return jnp.concatenate([occ_ref[:, y, :] for y in range(8)], axis=1).astype(F32)


def side_by_side(quad):
    v0, v1, v2, v3 = (v.astype(BF16).astype(F32) for v in quad)
    v1, v2, v3 = pltpu.roll(v1, 96, 1), pltpu.roll(v2, 64, 1), pltpu.roll(v3, 32, 1)
    lane = lax.broadcasted_iota(jnp.int32, v0.shape, 1)
    return jnp.concatenate([jnp.where(lane < 96, v0, v1), jnp.where(lane < 64, v1, v2), jnp.where(lane < 32, v2, v3)],
                           axis=1).astype(BF16)


def start_all(pairs, sems, first=0):
    copies = [pltpu.make_async_copy(src, dst, sems.at[first + i]) for i, (src, dst) in enumerate(pairs)]
    for copy in copies:
        copy.start()
    return copies


def up_kernel(sizes, occ_hbm, p6_hbm, p5_hbm, p4_hbm, gs_hbm, comp_hbm, x_hbm, s_hbm, kt_hbm,
              zs_hbm, g_hbm, p4t_hbm, p5t_hbm, exp_hbm,
              h6, r54, kp, mask6, mask5, mask4, zs_ref, g_ref, p4t_ref, p5t_ref, exp_ref, sv,
              occ_ref, p6_ref, p5_ref, p4_ref, gs_ref, comp_ref, xv, kt, mcat, comp, m5cat, msg, turned,
              const_sem, in_sem, kt_sem, send6, recv6, send54, recv54):
    gx, gy = lax.axis_index("gx"), lax.axis_index("gy")

    def there(ex, ey):
        ok = jnp.bool_(True)
        if ex:
            ok = (gx + ex >= 0) & (gx + ex < sizes[0])
        if ey:
            ok = ok & (gy + ey >= 0) & (gy + ey < sizes[1])
        return ok

    urgent = start_all([(comp_hbm, comp_ref), (occ_hbm, occ_ref), (p6_hbm, p6_ref)], const_sem)
    loads = start_all([(x_hbm.at[i], xv.at[i]) for i in range(8)], in_sem)

    zero = jnp.zeros((6, 16, 768), BF16)
    h6[0] = zero
    h6[5] = zero
    h6[1:5, 0] = zero[:4]
    h6[1:5, 5] = zero[:4]
    r54[48:240] = jnp.zeros((192, 768), BF16)
    barrier = pltpu.get_barrier_semaphore()
    for ex, ey in DIRS:
        @pl.when(there(ex, ey))
        def _():
            pl.semaphore_signal(barrier, inc=1, device_id=(gx + ex, gy + ey), device_id_type=MESH)

    for copy in urgent:
        copy.wait()
    comp[...] = jnp.concatenate([comp_ref[...].astype(F32), jnp.zeros((128 - RANK, NC), F32)], axis=0).T.astype(BF16)

    occ = occupied_rows(occ_ref)
    p6 = p6_ref[...].astype(F32)
    for x in range(8):
        loads[x].wait()
        if x == SECOND_AT:
            second = start_all([(s_hbm, sv), (p5_hbm, p5_ref), (p4_hbm, p4_ref), (gs_hbm, gs_ref)], const_sem, 3)
        masked = (p6 * occ[x:x + 1, :]).astype(BF16)
        rows = dot(masked, xv[x]).astype(BF16)
        for q in range(4):
            c = (x % 2) * 4 + q
            mcat[(x // 2) * 64:(x // 2) * 64 + 64, c * NC:(c + 1) * NC] = rows[q * 64:(q + 1) * 64]

    third = start_all([(kt_hbm.at[pl.ds(i * 16, 16)], kt.at[pl.ds(i * 16, 16)]) for i in range(6)], kt_sem)
    third += start_all([(zs_hbm, zs_ref), (g_hbm, g_ref), (p4t_hbm, p4t_ref), (p5t_hbm, p5t_ref),
                       (exp_hbm, exp_ref)], const_sem, 7)

    for h in range(2):
        charges = side_by_side([dot(mcat[:, c * NC:(c + 1) * NC], comp[...]) for c in range(4 * h, 4 * h + 4)])
        h6[1:5, 1:5, :, h * 384:(h + 1) * 384] = charges.reshape(4, 4, 16, 384)

    pl.semaphore_wait(barrier, sum(jnp.where(there(ex, ey), 1, 0) for ex, ey in DIRS))

    def part(e):
        return pl.ds(1, 4) if e == 0 else 4 if e > 0 else 1

    def landing(e):
        return pl.ds(1, 4) if e == 0 else 0 if e > 0 else 5

    fine = []
    for d, (ex, ey) in enumerate(DIRS):
        fine.append(pltpu.make_async_remote_copy(
            src_ref=h6.at[part(ex), part(ey)], dst_ref=h6.at[landing(ex), landing(ey)], send_sem=send6.at[d],
            recv_sem=recv6.at[d], device_id=(gx + ex, gy + ey), device_id_type=MESH))

        @pl.when(there(ex, ey))
        def _():
            fine[d].start()

    for copy in second:
        copy.wait()
    shifts = sv[...].reshape(8 * NC, NC)
    mid = dot(mcat[...], shifts).astype(BF16)
    mid = dot(p5_ref[...], mid).astype(BF16)
    for c in range(8):
        m5cat[:, c * NC:(c + 1) * NC] = mid[c * 32:(c + 1) * 32]
    q5 = dot(mid, comp[...])
    top = dot(m5cat[...], shifts).astype(BF16)
    top = dot(p4_ref[...], top).astype(BF16)
    q4 = dot(top, comp[...])
    for h in range(2):
        of = range(4 * h, 4 * h + 4)
        r54[0:32, h * 384:(h + 1) * 384] = side_by_side([q5[c * 32:(c + 1) * 32] for c in of])
        r54[32:48, h * 384:(h + 1) * 384] = side_by_side([q4[c * 16:(c + 1) * 16] for c in of])
    msg[...] = dot(gs_ref[...], r54[0:48]).astype(BF16)

    small = []
    for d, (ex, ey) in enumerate(DIRS):
        small.append(pltpu.make_async_remote_copy(
            src_ref=msg.at[pl.ds(PACK_AT[d], PACK[d])], dst_ref=r54.at[pl.ds(48 + PACK_AT[d], PACK[d])],
            send_sem=send54.at[d], recv_sem=recv54.at[d], device_id=(gx + ex, gy + ey), device_id_type=MESH))

        @pl.when(there(ex, ey))
        def _():
            small[d].start()

    ones = jnp.ones((256, 128), BF16)
    for x in range(8):
        rows = dot((p6 * occ[x:x + 1, :]).astype(BF16), ones)
        for q in range(4):
            mask6[(x % 2) * 4 + q, (x // 2) * 64:(x // 2) * 64 + 64] = rows[q * 64:(q + 1) * 64]
    top5 = mask6[0]
    for c in range(1, 8):
        top5 = jnp.maximum(top5, mask6[c])
    mask5[...] = top5
    by_class = dot(p5_ref[...], top5.astype(BF16))
    top4 = by_class[0:32]
    for c in range(1, 8):
        top4 = jnp.maximum(top4, by_class[c * 32:(c + 1) * 32])
    mask4[...] = top4

    for copy in third:
        copy.wait()

    @pl.loop(0, RANK, unroll=8)
    def _(r):
        v = jnp.concatenate([kt[r], jnp.zeros((128 - RANK, 316), BF16)], axis=0)
        v = jnp.concatenate([v, jnp.zeros((128, 68), BF16)], axis=1)
        turned[pl.ds(pl.multiple_of(r * STEP, 8), 320)] = v.T[:320].astype(F32)

    def taken(n, part):
        return turned[pl.ds(n + part * 32 * STEP, 32, stride=STEP), :]

    def blocks(bc, part, planes):
        for which, (low, even, high) in planes.items():
            rows = pl.ds(part * 32, 32)
            kp[which * 49 + bc, rows] = even.astype(BF16)
            kp[(3 + which) * 49 + bc, rows] = (high if which == 1 else high - even).astype(BF16)
            kp[(6 + which) * 49 + bc, rows] = (low if which == 1 else low - even).astype(BF16)

    for bc, outer, count in ((0, 0, 16), (19, 16, 4), (26, 20, 4), (33, 24, 16)):
        @pl.loop(0, count, unroll=2)
        def _(j):
            for part in range(3):
                p = [taken(n + j, part) for n in (bc, 49 + bc, 98 + outer, 138 + outer, 178 + outer, 218 + bc, 267 + bc)]
                blocks(bc + j, part, {0: p[0:3], 1: p[2:5], 2: p[4:7]})
    for bc in (16, 17, 18, 23, 24, 25, 30, 31, 32):
        for part in range(3):
            none = jnp.zeros((32, 128), F32)
            blocks(bc, part, {0: (taken(bc, part), taken(49 + bc, part), none),
                                   2: (none, taken(218 + bc, part), taken(267 + bc, part))})

    for copies in (fine, small):
        for d, (ex, ey) in enumerate(DIRS):
            @pl.when(there(ex, ey))
            def _():
                copies[d].wait_send()

            @pl.when(there(-ex, -ey))
            def _():
                copies[d].wait_recv()


def down_kernel(h6, r54, kp, mask6, mask5, mask4, zs_ref, g_ref, p4t_ref, p5t_ref, exp_ref, sv, out_hbm,
                hz, small, added, small_added, far, expp, mid_cm, mid_nat, ov, out_sem):

    for first, count in ((0, 16), (16, 16), (32, 4)):
        block = h6[first * 16:(first + count) * 16]
        hz[1, first * 16:(first + count) * 16] = block
        for k in range(2):
            hz[2 * k, first * 16:(first + count) * 16] = dot(
                zs_ref[k, 0:count * 16, 0:count * 16], block).astype(BF16)
    for i in range(6):
        small[i * 208:(i + 1) * 208] = dot(g_ref[i * 208:(i + 1) * 208], r54[...]).astype(BF16)

    def halves_added(v):
        return (v[:, 0:384].astype(F32) + v[:, 384:768].astype(F32)).astype(BF16)

    for i in range(3):
        added[i] = halves_added(hz[i])
    small_added[...] = halves_added(small[...])

    def window(i, kind):
        sx, sy, sz = (v + 1 for v in SHIFTS[i])
        grid, rows, cols = (added, small_added, slice(0, 384)) if kind == 0 else (
            hz, small, slice(384, 768) if kind == 1 else slice(0, 384))
        parts = [grid[sz, ((sx + x) * 6 + sy) * 16:((sx + x) * 6 + sy) * 16 + 64, cols] for x in range(4)]
        return jnp.concatenate(parts + [rows[i * SMALL_ROWS:(i + 1) * SMALL_ROWS, cols]], axis=0)

    def block(i, kind, s, t):
        sx, sy, sz = SHIFTS[i]
        b, c = 2 * sy + s // 2 - t // 2, 2 * sz + s % 2 - t % 2
        if sx == 0 and max(abs(b), abs(c)) < 2:
            return jnp.zeros((RANK, 128), BF16)
        return kp[(3 * kind + sx + 1) * 49 + (b + 3) * 7 + c + 3]

    def add(kind, pair, lhs, weights, start):
        cols = slice(pair * 256, (pair + 1) * 256)
        product = dot(lhs, jnp.concatenate([jnp.concatenate([w(2 * pair), w(2 * pair + 1)], axis=1) for w in weights], axis=0))
        if not start:
            product += far[kind, :, cols]
        far[kind, :, cols] = product

    aside = [i for i in range(26) if SHIFTS[i][0]]
    for first in range(0, len(aside), 2):
        two = aside[first:first + 2]
        for kind in range(3):
            lhs = jnp.concatenate([window(i, kind) for i in two], axis=1)
            for pair in range(2):
                add(kind, pair, lhs, [functools.partial(block, i, kind, s) for i in two for s in range(4)], first == 0)
    for i in range(26):
        if SHIFTS[i][0] == 0:
            lhs = jnp.concatenate([window(i, 2), window(i, 1)], axis=1)
            for kind, halves in ((1, (0, 1)), (2, (2, 0))):
                for pair in range(2):
                    add(kind, pair, lhs, [functools.partial(block, i, k, s) for k in halves for s in range(4)], False)

    def far_of(c, rows):
        cols = slice(c % 4 * 128, c % 4 * 128 + 128)
        return (far[0, rows, cols] + far[1 + c // 4, rows, cols]).astype(BF16)

    expp[...] = jnp.zeros_like(expp)
    expp[0:RANK] = exp_ref[...]
    expand = expp[...]
    wide = lambda m: jnp.concatenate([m] * 4, axis=1)
    f4 = jnp.concatenate([far_of(c, slice(288, 304)) for c in range(8)], axis=0)
    local4 = dot(p4t_ref[...], dot(f4, expand).astype(BF16))
    local4 = (local4 * wide(mask4[...])).astype(BF16)
    f5 = jnp.concatenate([far_of(c, slice(256, 288)) for c in range(8)], axis=0)
    mid_far = dot(f5, expand)
    for c in range(8):
        mid_cm[c * 32:(c + 1) * 32] = (mid_far[c * 32:(c + 1) * 32] + dot_t(local4, sv[c])).astype(BF16)
    mid_nat[...] = (dot(p5t_ref[...], mid_cm[...]) * wide(mask5[...])).astype(BF16)
    stores = []
    for c, (dx, dy, dz) in enumerate(BITS):
        v = dot_t(mid_nat[...], sv[c]) + dot(far_of(c, slice(0, 256)), expand)
        v = v * wide(mask6[c])
        for x in range(4):
            for y in range(4):
                for g in range(4):
                    ov[c // 2, g, x, y, pl.ds(dz, 16, stride=2), :] = v[(x * 4 + y) * 16:(x * 4 + y + 1) * 16,
                                                                       g * 128:(g + 1) * 128]
        if dz == 1:
            for g in range(4):
                stores.append(pltpu.make_async_copy(ov.at[c // 2, g], out_hbm.at[:, dx, :, dy, :, pl.ds(g * 128, 128)],
                                                    out_sem.at[c // 2 * 4 + g]))
                stores[-1].start()
    for store in stores:
        store.wait()


def full():
    return pl.BlockSpec(memory_space=pltpu.VMEM)


def held(array):
    return pltpu.with_memory_space_constraint(array, pltpu.HBM)


def in_hbm():
    return pl.BlockSpec(memory_space=pltpu.HBM)


def per_device(sizes, multipoles, occupied, shift_matrices, compress, kernels, expand):
    x = multipoles.reshape(8, 256, NC)
    p5, p4 = order_mid(), order_top()
    dma, vmem, shape = pltpu.SemaphoreType.DMA, pltpu.VMEM, pltpu.VMEM
    kept = pl.pallas_call(
        functools.partial(up_kernel, sizes),
        out_shape=(shape((6, 6, 16, 768), BF16), shape((240, 768), BF16), shape((441, RANK, 128), BF16),
                   shape((8, 256, 128), F32), shape((256, 128), F32), shape((32, 128), F32),
                   shape((2, 256, 256), BF16), shape((26 * SMALL_ROWS, 240), BF16), shape((32, 128), BF16),
                   shape((256, 256), BF16), shape((RANK, NC), BF16), shape((8, NC, NC), BF16)),
        in_specs=[in_hbm()] * 14,
        out_specs=(full(),) * 12,
        scratch_shapes=[
            vmem((8, 8, 32), jnp.int32), vmem((256, 256), BF16), vmem((256, 256), BF16), vmem((128, 32), BF16),
            vmem((192, 48), BF16), vmem((RANK, NC), BF16), vmem((8, 256, NC), BF16),
            vmem((RANK, RANK, 316), BF16), vmem((256, 8 * NC), BF16), vmem((NC, 128), BF16),
            vmem((32, 8 * NC), BF16), vmem((192, 768), BF16), vmem((RANK * STEP, 128), F32),
            dma((12,)), dma((8,)), dma((6,)), dma((8,)), dma((8,)), dma((8,)), dma((8,))],
        compiler_params=pltpu.CompilerParams(collective_id=0, has_side_effects=True, vmem_limit_bytes=34 * 2**20),
        name="up",
    )(*map(held, (occupied, const(order_fine()), const(p5), const(p4), const(packing()), compress.T, x,
                  shift_matrices, kernels.transpose(1, 2, 0), const(shift_z()), const(windows_small()), const(p4.T),
                  const(p5.T), expand)))

    out = pl.pallas_call(
        down_kernel,
        out_shape=jax.ShapeDtypeStruct((4, 2, 4, 2, 32, NC), F32),
        in_specs=[full()] * 12,
        out_specs=in_hbm(),
        scratch_shapes=[
            vmem((3, 576, 768), BF16), vmem((26 * SMALL_ROWS, 768), BF16), vmem((3, 576, 384), BF16),
            vmem((26 * SMALL_ROWS, 384), BF16), vmem((3, 304, 512), F32), vmem((128, NC), BF16), vmem((256, NC), BF16),
            vmem((256, NC), BF16), vmem((4, 4, 4, 4, 32, 128), F32), dma((16,))],
        compiler_params=pltpu.CompilerParams(vmem_limit_bytes=24 * 2**20),
        name="down",
    )(kept[0].reshape(576, 768), *kept[1:])
    return out.reshape(8, 8, 32, NC)


def solution(mesh):
    in_specs = (P("gx", "gy", None, None), P("gx", "gy", None), P(), P(), P(), P())
    out_specs = P("gx", "gy", None, None)
    sizes = (mesh.shape["gx"], mesh.shape["gy"])
    return jax.shard_map(
        functools.partial(per_device, sizes), mesh=mesh, in_specs=in_specs, out_specs=out_specs, check_vma=False
    )
```

```python
import functools

import jax
import jax.numpy as jnp
import ml_dtypes
import numpy as np
from jax import lax
from jax.experimental import pallas as pl
from jax.experimental.pallas import tpu as pltpu
from jax.sharding import PartitionSpec as P

MESH = pl.DeviceIdType.MESH
F32, BF16 = jnp.float32, jnp.bfloat16
NC, RANK = 512, 96
BITS = [(c // 4, c // 2 % 2, c % 2) for c in range(8)]
DIRS = [(-1, 0), (1, 0), (0, -1), (0, 1), (-1, -1), (-1, 1), (1, -1), (1, 1)]
PACK = [32, 32, 32, 32, 16, 16, 16, 16]
PACK_AT = [0, 32, 64, 96, 128, 144, 160, 176]
SMALL_ROWS = 48
STEP = 328
SHIFTS = [(a, b, c) for a in (-1, 0, 1) for b in (-1, 0, 1) for c in (-1, 0, 1) if (a, b, c) != (0, 0, 0)]


def dot(a, b):
    return jnp.dot(a, b, preferred_element_type=F32)


def dot_t(a, b):
    return lax.dot_general(a, b, (((1,), (1,)), ((), ())), preferred_element_type=F32)


def order_fine():
    row, col = (lax.broadcasted_iota(jnp.int32, (256, 256), k) for k in range(2))
    return jnp.where(col == row // 16 % 4 * 64 + row // 128 * 32 + row % 16 * 2 + row // 64 % 2, 1.0, 0.0)


def order_mid():
    p = np.zeros((256, 256), np.float32)
    for c, (dx, dy, dz) in enumerate(BITS):
        for x in range(2):
            for y in range(2):
                for z in range(8):
                    p[c * 32 + x * 16 + y * 8 + z, ((2 * x + dx) * 4 + 2 * y + dy) * 16 + 2 * z + dz] = 1
    return p


def order_top():
    p = np.zeros((128, 32), np.float32)
    for c, (dx, dy, dz) in enumerate(BITS):
        for z in range(4):
            p[c * 16 + z, (dx * 2 + dy) * 8 + 2 * z + dz] = 1
    return p


def packing():
    p = np.zeros((192, 48), np.float32)
    for (ex, ey), at in zip(DIRS, PACK_AT):
        if ex and ey:
            for z in range(8):
                p[at + z, (ex > 0) * 16 + (ey > 0) * 8 + z] = 1
            for z in range(4):
                p[at + 8 + z, 32 + z] = 1
        else:
            for w in range(2):
                for z in range(8):
                    x, y = ((ex > 0), w) if ex else (w, (ey > 0))
                    p[at + w * 8 + z, x * 16 + y * 8 + z] = 1
            for z in range(4):
                p[at + 16 + z, 32 + z] = 1
    return p


def windows_small():
    g = np.zeros((26, SMALL_ROWS, 240), np.float32)
    for i, (sx, sy, sz) in enumerate(SHIFTS):
        for x in range(2):
            for y in range(2):
                for z in range(8):
                    u, v, w = x + sx, y + sy, z + sz
                    if not 0 <= w < 8:
                        continue
                    ex, ey = (u > 1) - (u < 0), (v > 1) - (v < 0)
                    row = x * 16 + y * 8 + z
                    if not ex and not ey:
                        g[i, row, u * 16 + v * 8 + w] = 1
                        continue
                    at = 48 + PACK_AT[DIRS.index((-ex, -ey))]
                    g[i, row, at + (w if ex and ey else v * 8 + w if ex else u * 8 + w)] = 1
        for z in range(4):
            w = z + sz
            if not 0 <= w < 4:
                continue
            if not sx and not sy:
                g[i, 32 + z, 32 + w] = 1
            else:
                g[i, 32 + z, 48 + PACK_AT[DIRS.index((-sx, -sy))] + (8 if sx and sy else 16) + w] = 1
    return g.reshape(26 * SMALL_ROWS, 240)


def shift_z():
    p = np.zeros((2, 256, 256), np.float32)
    for k, s in enumerate((-1, 1)):
        for column in range(16):
            for z in range(16):
                if 0 <= z + s < 16:
                    p[k, column * 16 + z, column * 16 + z + s] = 1
    return p


def const(a):
    return jnp.asarray(a.astype(ml_dtypes.bfloat16))


def occupied_rows(occ_ref):
    return jnp.concatenate([occ_ref[:, y, :] for y in range(8)], axis=1).astype(F32)


def side_by_side(quad):
    v0, v1, v2, v3 = (v.astype(BF16).astype(F32) for v in quad)
    v1, v2, v3 = pltpu.roll(v1, 96, 1), pltpu.roll(v2, 64, 1), pltpu.roll(v3, 32, 1)
    lane = lax.broadcasted_iota(jnp.int32, v0.shape, 1)
    return jnp.concatenate([jnp.where(lane < 96, v0, v1), jnp.where(lane < 64, v1, v2), jnp.where(lane < 32, v2, v3)],
                           axis=1).astype(BF16)


def start_all(pairs, sems, first=0):
    copies = [pltpu.make_async_copy(src, dst, sems.at[first + i]) for i, (src, dst) in enumerate(pairs)]
    for copy in copies:
        copy.start()
    return copies


def up_kernel(sizes, occ_hbm, p5_hbm, p4_hbm, gs_hbm, comp_hbm, x_hbm, s_hbm, kt_hbm,
              zs_hbm, g_hbm, p4t_hbm, p5t_hbm, exp_hbm,
              h6, r54, kp, mask6, mask5, mask4, zs_ref, g_ref, p4t_ref, p5t_ref, exp_ref, sv,
              occ_ref, p5_ref, p4_ref, gs_ref, comp_ref, xv, kt, mcat, comp, m5cat, msg, turned,
              const_sem, in_sem, kt_sem, send6, recv6, send54, recv54):
    gx, gy = lax.axis_index("gx"), lax.axis_index("gy")

    def there(ex, ey):
        ok = jnp.bool_(True)
        if ex:
            ok = (gx + ex >= 0) & (gx + ex < sizes[0])
        if ey:
            ok = ok & (gy + ey >= 0) & (gy + ey < sizes[1])
        return ok

    urgent = start_all([(comp_hbm, comp_ref), (occ_hbm, occ_ref)], const_sem)
    loads = start_all([(x_hbm.at[pl.ds(4 * i, 4)], xv.at[pl.ds(4 * i, 4)]) for i in range(2)], in_sem)

    zero = jnp.zeros((6, 16, 768), BF16)
    h6[0] = zero
    h6[5] = zero
    h6[1:5, 0] = zero[:4]
    h6[1:5, 5] = zero[:4]
    r54[48:240] = jnp.zeros((192, 768), BF16)
    barrier = pltpu.get_barrier_semaphore()
    for ex, ey in DIRS:
        @pl.when(there(ex, ey))
        def _():
            pl.semaphore_signal(barrier, inc=1, device_id=(gx + ex, gy + ey), device_id_type=MESH)

    for copy in urgent:
        copy.wait()
    comp[...] = jnp.concatenate([comp_ref[...].astype(F32), jnp.zeros((128 - RANK, NC), F32)], axis=0).T.astype(BF16)

    occ = occupied_rows(occ_ref)
    p6 = order_fine()
    for x in range(8):
        if x % 4 == 0:
            loads[x // 4].wait()
        if x == 0:
            second = start_all([(s_hbm, sv), (p5_hbm, p5_ref), (p4_hbm, p4_ref), (gs_hbm, gs_ref)], const_sem, 2)
        masked = (p6 * occ[x:x + 1, :]).astype(BF16)
        rows = dot(masked, xv[x]).astype(BF16)
        for q in range(4):
            c = (x % 2) * 4 + q
            mcat[(x // 2) * 64:(x // 2) * 64 + 64, c * NC:(c + 1) * NC] = rows[q * 64:(q + 1) * 64]

    third = start_all([(kt_hbm.at[pl.ds(i * 16, 16)], kt.at[pl.ds(i * 16, 16)]) for i in range(6)], kt_sem)
    third += start_all([(zs_hbm, zs_ref), (g_hbm, g_ref), (p4t_hbm, p4t_ref), (p5t_hbm, p5t_ref),
                       (exp_hbm, exp_ref)], const_sem, 6)

    for h in range(2):
        charges = side_by_side([dot(mcat[:, c * NC:(c + 1) * NC], comp[...]) for c in range(4 * h, 4 * h + 4)])
        h6[1:5, 1:5, :, h * 384:(h + 1) * 384] = charges.reshape(4, 4, 16, 384)

    pl.semaphore_wait(barrier, sum(jnp.where(there(ex, ey), 1, 0) for ex, ey in DIRS))

    def part(e):
        return pl.ds(1, 4) if e == 0 else 4 if e > 0 else 1

    def landing(e):
        return pl.ds(1, 4) if e == 0 else 0 if e > 0 else 5

    fine = []
    for d, (ex, ey) in enumerate(DIRS):
        fine.append(pltpu.make_async_remote_copy(
            src_ref=h6.at[part(ex), part(ey)], dst_ref=h6.at[landing(ex), landing(ey)], send_sem=send6.at[d],
            recv_sem=recv6.at[d], device_id=(gx + ex, gy + ey), device_id_type=MESH))

        @pl.when(there(ex, ey))
        def _():
            fine[d].start()

    for copy in second:
        copy.wait()
    shifts = sv[...].reshape(8 * NC, NC)
    mid = dot(mcat[...], shifts).astype(BF16)
    mid = dot(p5_ref[...], mid).astype(BF16)
    for c in range(8):
        m5cat[:, c * NC:(c + 1) * NC] = mid[c * 32:(c + 1) * 32]
    q5 = dot(mid, comp[...])
    top = dot(m5cat[...], shifts).astype(BF16)
    top = dot(p4_ref[...], top).astype(BF16)
    q4 = dot(top, comp[...])
    for h in range(2):
        of = range(4 * h, 4 * h + 4)
        r54[0:32, h * 384:(h + 1) * 384] = side_by_side([q5[c * 32:(c + 1) * 32] for c in of])
        r54[32:48, h * 384:(h + 1) * 384] = side_by_side([q4[c * 16:(c + 1) * 16] for c in of])
    msg[...] = dot(gs_ref[...], r54[0:48]).astype(BF16)

    small = []
    for d, (ex, ey) in enumerate(DIRS):
        small.append(pltpu.make_async_remote_copy(
            src_ref=msg.at[pl.ds(PACK_AT[d], PACK[d])], dst_ref=r54.at[pl.ds(48 + PACK_AT[d], PACK[d])],
            send_sem=send54.at[d], recv_sem=recv54.at[d], device_id=(gx + ex, gy + ey), device_id_type=MESH))

        @pl.when(there(ex, ey))
        def _():
            small[d].start()

    ones = jnp.ones((256, 128), BF16)
    for x in range(8):
        rows = dot((p6 * occ[x:x + 1, :]).astype(BF16), ones)
        for q in range(4):
            mask6[(x % 2) * 4 + q, (x // 2) * 64:(x // 2) * 64 + 64] = rows[q * 64:(q + 1) * 64]
    top5 = mask6[0]
    for c in range(1, 8):
        top5 = jnp.maximum(top5, mask6[c])
    mask5[...] = top5
    by_class = dot(p5_ref[...], top5.astype(BF16))
    top4 = by_class[0:32]
    for c in range(1, 8):
        top4 = jnp.maximum(top4, by_class[c * 32:(c + 1) * 32])
    mask4[...] = top4

    for copy in third:
        copy.wait()

    @pl.loop(0, RANK, unroll=16)
    def _(r):
        v = jnp.concatenate([kt[r], jnp.zeros((128 - RANK, 316), BF16)], axis=0)
        v = jnp.concatenate([v, jnp.zeros((128, 68), BF16)], axis=1)
        turned[pl.ds(pl.multiple_of(r * STEP, 8), 320)] = v.T[:320].astype(F32)

    def taken(n, part):
        return turned[pl.ds(n + part * 32 * STEP, 32, stride=STEP), :]

    def blocks(bc, part, planes):
        for which, (low, even, high) in planes.items():
            rows = pl.ds(part * 32, 32)
            kp[which * 49 + bc, rows] = even.astype(BF16)
            kp[(3 + which) * 49 + bc, rows] = (high if which == 1 else high - even).astype(BF16)
            kp[(6 + which) * 49 + bc, rows] = (low if which == 1 else low - even).astype(BF16)

    for bc, outer, count in ((0, 0, 16), (19, 16, 4), (26, 20, 4), (33, 24, 16)):
        @pl.loop(0, count, unroll=4)
        def _(j):
            for part in range(3):
                p = [taken(n + j, part) for n in (bc, 49 + bc, 98 + outer, 138 + outer, 178 + outer, 218 + bc, 267 + bc)]
                blocks(bc + j, part, {0: p[0:3], 1: p[2:5], 2: p[4:7]})
    for bc in (16, 17, 18, 23, 24, 25, 30, 31, 32):
        for part in range(3):
            none = jnp.zeros((32, 128), F32)
            blocks(bc, part, {0: (taken(bc, part), taken(49 + bc, part), none),
                                   2: (none, taken(218 + bc, part), taken(267 + bc, part))})

    for copies in (fine, small):
        for d, (ex, ey) in enumerate(DIRS):
            @pl.when(there(ex, ey))
            def _():
                copies[d].wait_send()

            @pl.when(there(-ex, -ey))
            def _():
                copies[d].wait_recv()


def down_kernel(h6, r54, kp, mask6, mask5, mask4, zs_ref, g_ref, p4t_ref, p5t_ref, exp_ref, sv, out_hbm,
                hz, small, added, small_added, far, expp, mid_cm, mid_nat, ov, out_sem):

    for first, count in ((0, 16), (16, 16), (32, 4)):
        block = h6[first * 16:(first + count) * 16]
        hz[1, first * 16:(first + count) * 16] = block
        for k in range(2):
            hz[2 * k, first * 16:(first + count) * 16] = dot(
                zs_ref[k, 0:count * 16, 0:count * 16], block).astype(BF16)
    for i in range(6):
        small[i * 208:(i + 1) * 208] = dot(g_ref[i * 208:(i + 1) * 208], r54[...]).astype(BF16)

    def halves_added(v):
        return (v[:, 0:384].astype(F32) + v[:, 384:768].astype(F32)).astype(BF16)

    for i in range(3):
        added[i] = halves_added(hz[i])
    small_added[...] = halves_added(small[...])

    def window(i, kind):
        sx, sy, sz = (v + 1 for v in SHIFTS[i])
        grid, rows, cols = (added, small_added, slice(0, 384)) if kind == 0 else (
            hz, small, slice(384, 768) if kind == 1 else slice(0, 384))
        parts = [grid[sz, ((sx + x) * 6 + sy) * 16:((sx + x) * 6 + sy) * 16 + 64, cols] for x in range(4)]
        return jnp.concatenate(parts + [rows[i * SMALL_ROWS:(i + 1) * SMALL_ROWS, cols]], axis=0)

    def block(i, kind, s, t):
        sx, sy, sz = SHIFTS[i]
        b, c = 2 * sy + s // 2 - t // 2, 2 * sz + s % 2 - t % 2
        if sx == 0 and max(abs(b), abs(c)) < 2:
            return jnp.zeros((RANK, 128), BF16)
        return kp[(3 * kind + sx + 1) * 49 + (b + 3) * 7 + c + 3]

    def add(kind, pair, lhs, weights, start):
        cols = slice(pair * 256, (pair + 1) * 256)
        product = dot(lhs, jnp.concatenate([jnp.concatenate([w(2 * pair), w(2 * pair + 1)], axis=1) for w in weights], axis=0))
        if not start:
            product += far[kind, :, cols]
        far[kind, :, cols] = product

    aside = [i for i in range(26) if SHIFTS[i][0]]
    for first in range(0, len(aside), 2):
        two = aside[first:first + 2]
        for kind in range(3):
            lhs = jnp.concatenate([window(i, kind) for i in two], axis=1)
            for pair in range(2):
                add(kind, pair, lhs, [functools.partial(block, i, kind, s) for i in two for s in range(4)], first == 0)
    for i in range(26):
        if SHIFTS[i][0] == 0:
            lhs = jnp.concatenate([window(i, 2), window(i, 1)], axis=1)
            for kind, halves in ((1, (0, 1)), (2, (2, 0))):
                for pair in range(2):
                    add(kind, pair, lhs, [functools.partial(block, i, k, s) for k in halves for s in range(4)], False)

    def far_of(c, rows):
        cols = slice(c % 4 * 128, c % 4 * 128 + 128)
        return (far[0, rows, cols] + far[1 + c // 4, rows, cols]).astype(BF16)

    expp[...] = jnp.zeros_like(expp)
    expp[0:RANK] = exp_ref[...]
    expand = expp[...]
    wide = lambda m: jnp.concatenate([m] * 4, axis=1)
    f4 = jnp.concatenate([far_of(c, slice(288, 304)) for c in range(8)], axis=0)
    local4 = dot(p4t_ref[...], dot(f4, expand).astype(BF16))
    local4 = (local4 * wide(mask4[...])).astype(BF16)
    f5 = jnp.concatenate([far_of(c, slice(256, 288)) for c in range(8)], axis=0)
    mid_far = dot(f5, expand)
    for c in range(8):
        mid_cm[c * 32:(c + 1) * 32] = (mid_far[c * 32:(c + 1) * 32] + dot_t(local4, sv[c])).astype(BF16)
    mid_nat[...] = (dot(p5t_ref[...], mid_cm[...]) * wide(mask5[...])).astype(BF16)
    stores = []
    for c, (dx, dy, dz) in enumerate(BITS):
        v = dot_t(mid_nat[...], sv[c]) + dot(far_of(c, slice(0, 256)), expand)
        v = v * wide(mask6[c])
        for x in range(4):
            for y in range(4):
                for g in range(4):
                    ov[c // 2, g, x, y, pl.ds(dz, 16, stride=2), :] = v[(x * 4 + y) * 16:(x * 4 + y + 1) * 16,
                                                                       g * 128:(g + 1) * 128]
        if dz == 1:
            for g in range(4):
                stores.append(pltpu.make_async_copy(ov.at[c // 2, g], out_hbm.at[:, dx, :, dy, :, pl.ds(g * 128, 128)],
                                                    out_sem.at[c // 2 * 4 + g]))
                stores[-1].start()
    for store in stores:
        store.wait()


def full():
    return pl.BlockSpec(memory_space=pltpu.VMEM)


def held(array):
    return pltpu.with_memory_space_constraint(array, pltpu.HBM)


def in_hbm():
    return pl.BlockSpec(memory_space=pltpu.HBM)


def per_device(sizes, multipoles, occupied, shift_matrices, compress, kernels, expand):
    x = multipoles.reshape(8, 256, NC)
    p5, p4 = order_mid(), order_top()
    dma, vmem, shape = pltpu.SemaphoreType.DMA, pltpu.VMEM, pltpu.VMEM
    kept = pl.pallas_call(
        functools.partial(up_kernel, sizes),
        out_shape=(shape((6, 6, 16, 768), BF16), shape((240, 768), BF16), shape((441, RANK, 128), BF16),
                   shape((8, 256, 128), F32), shape((256, 128), F32), shape((32, 128), F32),
                   shape((2, 256, 256), BF16), shape((26 * SMALL_ROWS, 240), BF16), shape((32, 128), BF16),
                   shape((256, 256), BF16), shape((RANK, NC), BF16), shape((8, NC, NC), BF16)),
        in_specs=[in_hbm()] * 13,
        out_specs=(full(),) * 12,
        scratch_shapes=[
            vmem((8, 8, 32), jnp.int32), vmem((256, 256), BF16), vmem((128, 32), BF16),
            vmem((192, 48), BF16), vmem((RANK, NC), BF16), vmem((8, 256, NC), BF16),
            vmem((RANK, RANK, 316), BF16), vmem((256, 8 * NC), BF16), vmem((NC, 128), BF16),
            vmem((32, 8 * NC), BF16), vmem((192, 768), BF16), vmem((RANK * STEP, 128), F32),
            dma((11,)), dma((2,)), dma((6,)), dma((8,)), dma((8,)), dma((8,)), dma((8,))],
        compiler_params=pltpu.CompilerParams(collective_id=0, has_side_effects=True, vmem_limit_bytes=34 * 2**20),
        name="up",
    )(*map(held, (occupied, const(p5), const(p4), const(packing()), compress.T, x,
                  shift_matrices, kernels.transpose(1, 2, 0), const(shift_z()), const(windows_small()), const(p4.T),
                  const(p5.T), expand)))

    out = pl.pallas_call(
        down_kernel,
        out_shape=jax.ShapeDtypeStruct((4, 2, 4, 2, 32, NC), F32),
        in_specs=[full()] * 12,
        out_specs=in_hbm(),
        scratch_shapes=[
            vmem((3, 576, 768), BF16), vmem((26 * SMALL_ROWS, 768), BF16), vmem((3, 576, 384), BF16),
            vmem((26 * SMALL_ROWS, 384), BF16), vmem((3, 304, 512), F32), vmem((128, NC), BF16), vmem((256, NC), BF16),
            vmem((256, NC), BF16), vmem((4, 4, 4, 4, 32, 128), F32), dma((16,))],
        compiler_params=pltpu.CompilerParams(vmem_limit_bytes=24 * 2**20),
        name="down",
    )(kept[0].reshape(576, 768), *kept[1:])
    return out.reshape(8, 8, 32, NC)


def solution(mesh):
    in_specs = (P("gx", "gy", None, None), P("gx", "gy", None), P(), P(), P(), P())
    out_specs = P("gx", "gy", None, None)
    sizes = (mesh.shape["gx"], mesh.shape["gy"])
    return jax.shard_map(
        functools.partial(per_device, sizes), mesh=mesh, in_specs=in_specs, out_specs=out_specs, check_vma=False
    )
```

```python
import functools

import jax
import jax.numpy as jnp
import ml_dtypes
import numpy as np
from jax import lax
from jax.experimental import pallas as pl
from jax.experimental.pallas import tpu as pltpu
from jax.sharding import PartitionSpec as P

MESH = pl.DeviceIdType.MESH
F32, BF16 = jnp.float32, jnp.bfloat16
NC, RANK = 512, 96
BITS = [(c // 4, c // 2 % 2, c % 2) for c in range(8)]
DIRS = [(-1, 0), (1, 0), (0, -1), (0, 1), (-1, -1), (-1, 1), (1, -1), (1, 1)]
PACK = [32, 32, 32, 32, 16, 16, 16, 16]
PACK_AT = [0, 32, 64, 96, 128, 144, 160, 176]
SMALL_ROWS = 48
STEP = 328
SHIFTS = [(a, b, c) for a in (-1, 0, 1) for b in (-1, 0, 1) for c in (-1, 0, 1) if (a, b, c) != (0, 0, 0)]


def dot(a, b):
    return jnp.dot(a, b, preferred_element_type=F32)


def dot_t(a, b):
    return lax.dot_general(a, b, (((1,), (1,)), ((), ())), preferred_element_type=F32)


def order_fine():
    row, col = (lax.broadcasted_iota(jnp.int32, (256, 256), k) for k in range(2))
    return jnp.where(col == row // 16 % 4 * 64 + row // 128 * 32 + row % 16 * 2 + row // 64 % 2, 1.0, 0.0)


def order_mid():
    p = np.zeros((256, 256), np.float32)
    for c, (dx, dy, dz) in enumerate(BITS):
        for x in range(2):
            for y in range(2):
                for z in range(8):
                    p[c * 32 + x * 16 + y * 8 + z, ((2 * x + dx) * 4 + 2 * y + dy) * 16 + 2 * z + dz] = 1
    return p


def order_top():
    p = np.zeros((128, 32), np.float32)
    for c, (dx, dy, dz) in enumerate(BITS):
        for z in range(4):
            p[c * 16 + z, (dx * 2 + dy) * 8 + 2 * z + dz] = 1
    return p


def packing():
    p = np.zeros((192, 48), np.float32)
    for (ex, ey), at in zip(DIRS, PACK_AT):
        if ex and ey:
            for z in range(8):
                p[at + z, (ex > 0) * 16 + (ey > 0) * 8 + z] = 1
            for z in range(4):
                p[at + 8 + z, 32 + z] = 1
        else:
            for w in range(2):
                for z in range(8):
                    x, y = ((ex > 0), w) if ex else (w, (ey > 0))
                    p[at + w * 8 + z, x * 16 + y * 8 + z] = 1
            for z in range(4):
                p[at + 16 + z, 32 + z] = 1
    return p


def windows_small():
    g = np.zeros((26, SMALL_ROWS, 240), np.float32)
    for i, (sx, sy, sz) in enumerate(SHIFTS):
        for x in range(2):
            for y in range(2):
                for z in range(8):
                    u, v, w = x + sx, y + sy, z + sz
                    if not 0 <= w < 8:
                        continue
                    ex, ey = (u > 1) - (u < 0), (v > 1) - (v < 0)
                    row = x * 16 + y * 8 + z
                    if not ex and not ey:
                        g[i, row, u * 16 + v * 8 + w] = 1
                        continue
                    at = 48 + PACK_AT[DIRS.index((-ex, -ey))]
                    g[i, row, at + (w if ex and ey else v * 8 + w if ex else u * 8 + w)] = 1
        for z in range(4):
            w = z + sz
            if not 0 <= w < 4:
                continue
            if not sx and not sy:
                g[i, 32 + z, 32 + w] = 1
            else:
                g[i, 32 + z, 48 + PACK_AT[DIRS.index((-sx, -sy))] + (8 if sx and sy else 16) + w] = 1
    return g.reshape(26 * SMALL_ROWS, 240)


def shift_z():
    p = np.zeros((2, 256, 256), np.float32)
    for k, s in enumerate((-1, 1)):
        for column in range(16):
            for z in range(16):
                if 0 <= z + s < 16:
                    p[k, column * 16 + z, column * 16 + z + s] = 1
    return p


def const(a):
    return jnp.asarray(a.astype(ml_dtypes.bfloat16))


def occupied_rows(occ_ref):
    return jnp.concatenate([occ_ref[:, y, :] for y in range(8)], axis=1).astype(F32)


def side_by_side(quad):
    v0, v1, v2, v3 = (v.astype(BF16).astype(F32) for v in quad)
    v1, v2, v3 = pltpu.roll(v1, 96, 1), pltpu.roll(v2, 64, 1), pltpu.roll(v3, 32, 1)
    lane = lax.broadcasted_iota(jnp.int32, v0.shape, 1)
    return jnp.concatenate([jnp.where(lane < 96, v0, v1), jnp.where(lane < 64, v1, v2), jnp.where(lane < 32, v2, v3)],
                           axis=1).astype(BF16)


def start_all(pairs, sems, first=0):
    copies = [pltpu.make_async_copy(src, dst, sems.at[first + i]) for i, (src, dst) in enumerate(pairs)]
    for copy in copies:
        copy.start()
    return copies


def up_kernel(sizes, occ_hbm, p5_hbm, p4_hbm, gs_hbm, comp_hbm, x_hbm, s_hbm, kt_hbm,
              zs_hbm, g_hbm, p4t_hbm, p5t_hbm, exp_hbm,
              h6, r54, kp, mask6, mask5, mask4, zs_ref, g_ref, p4t_ref, p5t_ref, exp_ref, sv,
              occ_ref, p5_ref, p4_ref, gs_ref, comp_ref, xv, kt, mcat, comp, m5cat, msg, turned,
              const_sem, in_sem, kt_sem, send6, recv6, send54, recv54):
    gx, gy = lax.axis_index("gx"), lax.axis_index("gy")

    def there(ex, ey):
        ok = jnp.bool_(True)
        if ex:
            ok = (gx + ex >= 0) & (gx + ex < sizes[0])
        if ey:
            ok = ok & (gy + ey >= 0) & (gy + ey < sizes[1])
        return ok

    urgent = start_all([(comp_hbm, comp_ref), (occ_hbm, occ_ref)], const_sem)
    loads = start_all([(x_hbm.at[pl.ds(4 * i, 4)], xv.at[pl.ds(4 * i, 4)]) for i in range(2)], in_sem)

    zero = jnp.zeros((6, 16, 768), BF16)
    h6[0] = zero
    h6[5] = zero
    h6[1:5, 0] = zero[:4]
    h6[1:5, 5] = zero[:4]
    r54[48:240] = jnp.zeros((192, 768), BF16)
    barrier = pltpu.get_barrier_semaphore()
    for ex, ey in DIRS:
        @pl.when(there(ex, ey))
        def _():
            pl.semaphore_signal(barrier, inc=1, device_id=(gx + ex, gy + ey), device_id_type=MESH)

    for copy in urgent:
        copy.wait()
    comp[...] = jnp.concatenate([comp_ref[...].astype(F32), jnp.zeros((128 - RANK, NC), F32)], axis=0).T.astype(BF16)

    occ = occupied_rows(occ_ref)
    p6 = order_fine()
    for x in range(8):
        if x % 4 == 0:
            loads[x // 4].wait()
        if x == 0:
            second = start_all([(s_hbm, sv), (p5_hbm, p5_ref), (p4_hbm, p4_ref), (gs_hbm, gs_ref)], const_sem, 2)
        masked = (p6 * occ[x:x + 1, :]).astype(BF16)
        rows = dot(masked, xv[x]).astype(BF16)
        for q in range(4):
            c = (x % 2) * 4 + q
            mcat[(x // 2) * 64:(x // 2) * 64 + 64, c * NC:(c + 1) * NC] = rows[q * 64:(q + 1) * 64]

    third = start_all([(kt_hbm.at[pl.ds(i * 16, 16)], kt.at[pl.ds(i * 16, 16)]) for i in range(6)], kt_sem)
    third += start_all([(zs_hbm, zs_ref), (g_hbm, g_ref), (p4t_hbm, p4t_ref), (p5t_hbm, p5t_ref),
                       (exp_hbm, exp_ref)], const_sem, 6)

    for h in range(2):
        charges = side_by_side([dot(mcat[:, c * NC:(c + 1) * NC], comp[...]) for c in range(4 * h, 4 * h + 4)])
        h6[1:5, 1:5, :, h * 384:(h + 1) * 384] = charges.reshape(4, 4, 16, 384)

    pl.semaphore_wait(barrier, sum(jnp.where(there(ex, ey), 1, 0) for ex, ey in DIRS))

    def part(e):
        return pl.ds(1, 4) if e == 0 else 4 if e > 0 else 1

    def landing(e):
        return pl.ds(1, 4) if e == 0 else 0 if e > 0 else 5

    fine = []
    for d, (ex, ey) in enumerate(DIRS):
        fine.append(pltpu.make_async_remote_copy(
            src_ref=h6.at[part(ex), part(ey)], dst_ref=h6.at[landing(ex), landing(ey)], send_sem=send6.at[d],
            recv_sem=recv6.at[d], device_id=(gx + ex, gy + ey), device_id_type=MESH))

        @pl.when(there(ex, ey))
        def _():
            fine[d].start()

    for copy in second:
        copy.wait()
    shifts = sv[...].reshape(8 * NC, NC)
    mid = dot(mcat[...], shifts).astype(BF16)
    mid = dot(p5_ref[...], mid).astype(BF16)
    for c in range(8):
        m5cat[:, c * NC:(c + 1) * NC] = mid[c * 32:(c + 1) * 32]
    q5 = dot(mid, comp[...])
    top = dot(m5cat[...], shifts).astype(BF16)
    top = dot(p4_ref[...], top).astype(BF16)
    q4 = dot(top, comp[...])
    for h in range(2):
        of = range(4 * h, 4 * h + 4)
        r54[0:32, h * 384:(h + 1) * 384] = side_by_side([q5[c * 32:(c + 1) * 32] for c in of])
        r54[32:48, h * 384:(h + 1) * 384] = side_by_side([q4[c * 16:(c + 1) * 16] for c in of])
    msg[...] = dot(gs_ref[...], r54[0:48]).astype(BF16)

    small = []
    for d, (ex, ey) in enumerate(DIRS):
        small.append(pltpu.make_async_remote_copy(
            src_ref=msg.at[pl.ds(PACK_AT[d], PACK[d])], dst_ref=r54.at[pl.ds(48 + PACK_AT[d], PACK[d])],
            send_sem=send54.at[d], recv_sem=recv54.at[d], device_id=(gx + ex, gy + ey), device_id_type=MESH))

        @pl.when(there(ex, ey))
        def _():
            small[d].start()

    ones = jnp.ones((256, 128), BF16)
    for x in range(8):
        rows = dot((p6 * occ[x:x + 1, :]).astype(BF16), ones)
        for q in range(4):
            mask6[(x % 2) * 4 + q, (x // 2) * 64:(x // 2) * 64 + 64] = rows[q * 64:(q + 1) * 64]
    top5 = mask6[0]
    for c in range(1, 8):
        top5 = jnp.maximum(top5, mask6[c])
    mask5[...] = top5
    by_class = dot(p5_ref[...], top5.astype(BF16))
    top4 = by_class[0:32]
    for c in range(1, 8):
        top4 = jnp.maximum(top4, by_class[c * 32:(c + 1) * 32])
    mask4[...] = top4

    for copy in third:
        copy.wait()

    @pl.loop(0, RANK, unroll=16)
    def _(r):
        v = jnp.concatenate([kt[r], jnp.zeros((128 - RANK, 316), BF16)], axis=0)
        v = jnp.concatenate([v, jnp.zeros((128, 68), BF16)], axis=1)
        turned[pl.ds(pl.multiple_of(r * STEP, 8), 320)] = v.T[:320].astype(F32)

    def taken(n, part):
        return turned[pl.ds(n + part * 32 * STEP, 32, stride=STEP), :]

    def blocks(bc, part, planes):
        for which, (low, even, high) in planes.items():
            rows = pl.ds(part * 32, 32)
            kp[which * 49 + bc, rows] = even.astype(BF16)
            kp[(3 + which) * 49 + bc, rows] = (high if which == 1 else high - even).astype(BF16)
            kp[(6 + which) * 49 + bc, rows] = (low if which == 1 else low - even).astype(BF16)

    for bc, outer, count in ((0, 0, 16), (19, 16, 4), (26, 20, 4), (33, 24, 16)):
        @pl.loop(0, count, unroll=4)
        def _(j):
            for part in range(3):
                p = [taken(n + j, part) for n in (bc, 49 + bc, 98 + outer, 138 + outer, 178 + outer, 218 + bc, 267 + bc)]
                blocks(bc + j, part, {0: p[0:3], 1: p[2:5], 2: p[4:7]})
    for bc in (16, 17, 18, 23, 24, 25, 30, 31, 32):
        for part in range(3):
            none = jnp.zeros((32, 128), F32)
            blocks(bc, part, {0: (taken(bc, part), taken(49 + bc, part), none),
                                   2: (none, taken(218 + bc, part), taken(267 + bc, part))})

    for copies in (fine, small):
        for d, (ex, ey) in enumerate(DIRS):
            @pl.when(there(ex, ey))
            def _():
                copies[d].wait_send()

            @pl.when(there(-ex, -ey))
            def _():
                copies[d].wait_recv()


def down_kernel(h6, r54, kp, mask6, mask5, mask4, zs_ref, g_ref, p4t_ref, p5t_ref, exp_ref, sv, out_hbm,
                hz, small, added, small_added, far, expp, mid_cm, mid_nat, ov, out_sem):

    for first, count in ((0, 16), (16, 16), (32, 4)):
        block = h6[first * 16:(first + count) * 16]
        hz[1, first * 16:(first + count) * 16] = block
        for k in range(2):
            hz[2 * k, first * 16:(first + count) * 16] = dot(
                zs_ref[k, 0:count * 16, 0:count * 16], block).astype(BF16)
    for i in range(6):
        small[i * 208:(i + 1) * 208] = dot(g_ref[i * 208:(i + 1) * 208], r54[...]).astype(BF16)

    def halves_added(v):
        return (v[:, 0:384].astype(F32) + v[:, 384:768].astype(F32)).astype(BF16)

    for i in range(3):
        added[i] = halves_added(hz[i])
    small_added[...] = halves_added(small[...])

    def window(i, kind):
        sx, sy, sz = (v + 1 for v in SHIFTS[i])
        grid, rows, cols = (added, small_added, slice(0, 384)) if kind == 0 else (
            hz, small, slice(384, 768) if kind == 1 else slice(0, 384))
        parts = [grid[sz, ((sx + x) * 6 + sy) * 16:((sx + x) * 6 + sy) * 16 + 64, cols] for x in range(4)]
        return jnp.concatenate(parts + [rows[i * SMALL_ROWS:(i + 1) * SMALL_ROWS, cols]], axis=0)

    def block(i, kind, s, t):
        sx, sy, sz = SHIFTS[i]
        b, c = 2 * sy + s // 2 - t // 2, 2 * sz + s % 2 - t % 2
        if sx == 0 and max(abs(b), abs(c)) < 2:
            return jnp.zeros((RANK, 128), BF16)
        return kp[(3 * kind + sx + 1) * 49 + (b + 3) * 7 + c + 3]

    def add(kind, pair, lhs, weights, start):
        cols = slice(pair * 256, (pair + 1) * 256)
        product = dot(lhs, jnp.concatenate([jnp.concatenate([w(2 * pair), w(2 * pair + 1)], axis=1) for w in weights], axis=0))
        if not start:
            product += far[kind, :, cols]
        far[kind, :, cols] = product

    aside = [i for i in range(26) if SHIFTS[i][0]]
    for first in range(0, len(aside), 2):
        two = aside[first:first + 2]
        for kind in range(3):
            lhs = jnp.concatenate([window(i, kind) for i in two], axis=1)
            for pair in range(2):
                add(kind, pair, lhs, [functools.partial(block, i, kind, s) for i in two for s in range(4)], first == 0)
    for i in range(26):
        if SHIFTS[i][0] == 0:
            lhs = jnp.concatenate([window(i, 2), window(i, 1)], axis=1)
            for kind, halves in ((1, (0, 1)), (2, (2, 0))):
                for pair in range(2):
                    add(kind, pair, lhs, [functools.partial(block, i, k, s) for k in halves for s in range(4)], False)

    def far_of(c, rows):
        cols = slice(c % 4 * 128, c % 4 * 128 + 128)
        return (far[0, rows, cols] + far[1 + c // 4, rows, cols]).astype(BF16)

    expp[...] = jnp.zeros_like(expp)
    expp[0:RANK] = exp_ref[...]
    expand = expp[...]
    wide = lambda m: jnp.concatenate([m] * 4, axis=1)
    f4 = jnp.concatenate([far_of(c, slice(288, 304)) for c in range(8)], axis=0)
    local4 = dot(p4t_ref[...], dot(f4, expand).astype(BF16))
    local4 = (local4 * wide(mask4[...])).astype(BF16)
    f5 = jnp.concatenate([far_of(c, slice(256, 288)) for c in range(8)], axis=0)
    mid_far = dot(f5, expand)
    for c in range(8):
        mid_cm[c * 32:(c + 1) * 32] = (mid_far[c * 32:(c + 1) * 32] + dot_t(local4, sv[c])).astype(BF16)
    mid_nat[...] = (dot(p5t_ref[...], mid_cm[...]) * wide(mask5[...])).astype(BF16)
    stores = []
    for c, (dx, dy, dz) in enumerate(BITS):
        v = dot_t(mid_nat[...], sv[c]) + dot(far_of(c, slice(0, 256)), expand)
        v = v * wide(mask6[c])
        for x in range(4):
            for y in range(4):
                for g in range(4):
                    ov[c // 2, g, x, y, pl.ds(dz, 16, stride=2), :] = v[(x * 4 + y) * 16:(x * 4 + y + 1) * 16,
                                                                       g * 128:(g + 1) * 128]
        if dz == 1:
            for g in range(4):
                stores.append(pltpu.make_async_copy(ov.at[c // 2, g, :, :, pl.ds(0, 32)], out_hbm.at[:, dx, :, dy, :, pl.ds(g * 128, 128)],
                                                    out_sem.at[c // 2 * 4 + g]))
                stores[-1].start()
    for store in stores:
        store.wait()


def full():
    return pl.BlockSpec(memory_space=pltpu.VMEM)


def held(array):
    return pltpu.with_memory_space_constraint(array, pltpu.HBM)


def in_hbm():
    return pl.BlockSpec(memory_space=pltpu.HBM)


def per_device(sizes, multipoles, occupied, shift_matrices, compress, kernels, expand):
    x = multipoles.reshape(8, 256, NC)
    p5, p4 = order_mid(), order_top()
    dma, vmem, shape = pltpu.SemaphoreType.DMA, pltpu.VMEM, pltpu.VMEM
    kept = pl.pallas_call(
        functools.partial(up_kernel, sizes),
        out_shape=(shape((6, 6, 16, 768), BF16), shape((240, 768), BF16), shape((441, RANK, 128), BF16),
                   shape((8, 256, 128), F32), shape((256, 128), F32), shape((32, 128), F32),
                   shape((2, 256, 256), BF16), shape((26 * SMALL_ROWS, 240), BF16), shape((32, 128), BF16),
                   shape((256, 256), BF16), shape((RANK, NC), BF16), shape((8, NC, NC), BF16)),
        in_specs=[in_hbm()] * 13,
        out_specs=(full(),) * 12,
        scratch_shapes=[
            vmem((8, 8, 32), jnp.int32), vmem((256, 256), BF16), vmem((128, 32), BF16),
            vmem((192, 48), BF16), vmem((RANK, NC), BF16), vmem((8, 256, NC), BF16),
            vmem((RANK, RANK, 316), BF16), vmem((256, 8 * NC), BF16), vmem((NC, 128), BF16),
            vmem((32, 8 * NC), BF16), vmem((192, 768), BF16), vmem(((RANK + 1) * STEP, 128), F32),
            dma((11,)), dma((2,)), dma((6,)), dma((8,)), dma((8,)), dma((8,)), dma((8,))],
        compiler_params=pltpu.CompilerParams(collective_id=0, has_side_effects=True, vmem_limit_bytes=34 * 2**20),
        name="up",
    )(*map(held, (occupied, const(p5), const(p4), const(packing()), compress.T, x,
                  shift_matrices, kernels.transpose(1, 2, 0), const(shift_z()), const(windows_small()), const(p4.T),
                  const(p5.T), expand)))

    out = pl.pallas_call(
        down_kernel,
        out_shape=jax.ShapeDtypeStruct((4, 2, 4, 2, 32, NC), F32),
        in_specs=[full()] * 12,
        out_specs=in_hbm(),
        scratch_shapes=[
            vmem((3, 576, 768), BF16), vmem((26 * SMALL_ROWS, 768), BF16), vmem((3, 576, 384), BF16),
            vmem((26 * SMALL_ROWS, 384), BF16), vmem((3, 304, 512), F32), vmem((128, NC), BF16), vmem((256, NC), BF16),
            vmem((256, NC), BF16), vmem((4, 4, 4, 4, 40, 128), F32), dma((16,))],
        compiler_params=pltpu.CompilerParams(vmem_limit_bytes=24 * 2**20),
        name="down",
    )(kept[0].reshape(576, 768), *kept[1:])
    return out.reshape(8, 8, 32, NC)


def solution(mesh):
    in_specs = (P("gx", "gy", None, None), P("gx", "gy", None), P(), P(), P(), P())
    out_specs = P("gx", "gy", None, None)
    sizes = (mesh.shape["gx"], mesh.shape["gy"])
    return jax.shard_map(
        functools.partial(per_device, sizes), mesh=mesh, in_specs=in_specs, out_specs=out_specs, check_vma=False
    )
```
